256 devices in a mesh: src: 16 (over y_hi, z), freq: 16 (over x, y_lo, core).
Axes of the slice: x: 4, y: 4 (y_hi: 2, y_lo: 2; y = y_hi * 2 + y_lo), z: 8, core: 2. Of those that a mesh axis runs over, the one named last changes fastest.
Arguments:
- reflection: bfloat16 [2, 64, 2304, 2304], P(None, 'freq', 'src'), may hold values from -0.09375 to 0.09375
- focusing: bfloat16 [2, 64, 2304, 128], P(None, 'freq', 'src'), may hold values from -6 to 6
- direct_field: float32 [128, 2304, 128], P('freq', 'src'), may hold values from -6 to 6
- onset_index: int32 [2304, 128], P('src'), may hold values from 1 to 63
- end_index: int32 [2304, 128], P('src'), may hold values from 65 to 127
Outputs:
- updated: float32 [128, 2304, 128], P('freq', 'src')
The draws below stay inside these ranges and needn't reach their ends.
Inputs may be any that keep to these rules, and one draw needn't show every extreme that they name: `onset_index`: each trace's onset lies before the middle sample. `end_index`: each trace's window ends after the middle sample.
All inputs are finite; a program needn't handle non-finite values.
Results may differ from the reference program's by a relative error of at most 0.0003.
Values may be sent and summed in bfloat16 or wider, within the bound.
A program may use at most 64 MiB of HBM per device.

```python
import math
import jax
import jax.numpy as jnp
from jax import lax

NR = 2304
NS = 2304
NP = 128
RESIDUES = 16
FREQS = 64
NT = 128


def with_ends(entries, key, least, top_value):
    place = [jax.random.randint(jax.random.fold_in(key, axis), (), 0, length) for axis, length in enumerate(entries.shape)]
    longest = entries.shape.index(max(entries.shape))
    next_to = place[:longest] + [(place[longest] + 1) % entries.shape[longest]] + place[longest + 1:]
    return entries.at[tuple(place)].set(least).at[tuple(next_to)].set(top_value)


def levels(own_key, extent, shards, low, high):
    def one(dim, parts):
        steps = jax.random.uniform(jax.random.fold_in(jax.random.fold_in(own_key, 6), dim), (parts,), jnp.float32, low / len(shards), high / len(shards))
        return jnp.repeat(jnp.exp(steps), extent[dim] // parts).reshape((-1,) + (1,) * (len(extent) - dim - 1))

    gain = one(*shards[0])
    for cut in shards[1:]:
        gain = gain * one(*cut)
    return gain


def gaussian(own_key, shape, width, bound, split=(), kind=jnp.bfloat16):
    drawn = width * jax.random.normal(own_key, shape, jnp.float32)
    if split:
        drawn = drawn * levels(own_key, shape, split, -0.22, 0.18)
    return jnp.clip(drawn, -bound, bound).astype(kind)


def setup_inputs(seed: int = 0) -> dict:
    keys = jax.random.split(jax.random.key(seed), 6)
    return {
        "reflection": gaussian(keys[0], (2, FREQS, NR, NS), (2 * NS) ** -0.5, 0.09375, ((1, 16), (2, 16))),
        "focusing": gaussian(keys[1], (2, FREQS, NS, NP), 1.0, 6.0, ((1, 16), (2, 16))),
        "direct_field": gaussian(keys[2], (NT, NR, NP), 1.0, 6.0, ((0, 16), (1, 16)), jnp.float32),
        "onset_index": with_ends(jax.random.randint(keys[3], (NR, NP), 1, NT // 2), jax.random.fold_in(keys[3], 1), 1, (NT // 2) - 1).astype(jnp.int32),
        "end_index": with_ends(jax.random.randint(keys[4], (NR, NP), NT // 2 + 1, NT), jax.random.fold_in(keys[4], 1), NT // 2 + 1, NT - 1).astype(jnp.int32),
    }


def reverse_bits(values, bit_count):
    result = jnp.zeros_like(values)
    for bit_index in range(bit_count):
        result = result + values // 2 ** bit_index % 2 * 2 ** (bit_count - 1 - bit_index)
    return result

def reference(reflection, focusing, direct_field, onset_index, end_index):
    freq_total = reflection.shape[1]
    sample_total = 2 * freq_total
    bit_count = RESIDUES.bit_length() - 1
    per_device = freq_total // RESIDUES

    def one_frequency(freq_row):
        matrix = lax.dynamic_index_in_dim(reflection, freq_row, 1, keepdims=False)
        vector = lax.dynamic_index_in_dim(focusing, freq_row, 1, keepdims=False)
        real_part = jnp.dot(matrix[0], vector[0], preferred_element_type=jnp.float32) - jnp.dot(matrix[1], vector[1], preferred_element_type=jnp.float32)
        imag_part = jnp.dot(matrix[0], vector[1], preferred_element_type=jnp.float32) + jnp.dot(matrix[1], vector[0], preferred_element_type=jnp.float32)
        return jnp.stack((real_part, imag_part))
    freq_rows = jnp.arange(freq_total, dtype=jnp.int32)
    spectrum = lax.map(one_frequency, freq_rows)
    frequency = freq_rows % per_device * RESIDUES + reverse_bits(freq_rows // per_device, bit_count)
    samples = jnp.arange(sample_total, dtype=jnp.int32)
    phase_index = samples[:, None] * frequency[None, :] % sample_total
    twiddle_angle = phase_index.astype(jnp.float32) * (2.0 * math.pi / sample_total)
    norm_factor = 1.0 / math.sqrt(freq_total)
    trace = (jnp.einsum('sq,qrn->srn', jnp.cos(twiddle_angle), spectrum[:, 0], precision=lax.Precision.HIGHEST) - jnp.einsum('sq,qrn->srn', jnp.sin(twiddle_angle), spectrum[:, 1], precision=lax.Precision.HIGHEST)) * norm_factor
    window = (samples[:, None, None] >= onset_index[None]) & (samples[:, None, None] < end_index[None])
    muted = jnp.where(window, trace, jnp.float32(0.0))
    reversed_trace = jnp.roll(jnp.flip(muted, 0), 1, 0)
    return direct_field - reversed_trace
```

```python
import functools

import jax
import jax.numpy as jnp
import numpy as np
from jax import lax
from jax.experimental import pallas as pl
from jax.experimental.pallas import tpu as pltpu
from jax.sharding import PartitionSpec as P

MESH = pl.DeviceIdType.MESH

Z = 8
SRC = 16
FRQ = 16
L = 4
ROWS = 144
NPTS = 128
NSRC = SRC * ROWS
PER = ROWS // FRQ
PIECE = 24
BACK = PER * 8

A, B, ALL = (0, 128), (128, 128), (0, 256)
OWN, PAR = 0, 1
MOVES = (
    ("z+", OWN, -1, ALL),
    ("z+", OWN, -2, ALL),
    ("z+", OWN, -3, ALL),
    ("z+", OWN, -4, A),
    ("z+", PAR, -2, ALL),
    ("z+", PAR, -3, A),
    ("z-", OWN, 1, ALL),
    ("z-", OWN, 2, ALL),
    ("z-", OWN, 3, ALL),
    ("z-", OWN, 4, B),
    ("z-", PAR, 2, ALL),
    ("z-", PAR, 3, A),
    ("y", PAR, 0, ALL),
    ("y", PAR, -1, ALL),
    ("y", PAR, 1, ALL),
    ("y", PAR, -3, B),
    ("y", PAR, 3, B),
    ("y", PAR, 4, ALL),
)
ZP1, ZP2, ZP3, ZP4, ZQ2, ZQ3, ZM1, ZM2, ZM3, ZM4, ZN2, ZN3, Y0, YM1, YP1, YM3, YP3, Y4 = range(18)


def split(value):
    high = value.astype(jnp.bfloat16)
    return high, (value - high.astype(jnp.float32)).astype(jnp.bfloat16)


def kernel(
    refl, focus, direct, onset, ending, table,
    out,
    gath, mat, spec, got, trace, back, dir_v, on_v, end_v, tab_v, tab3, out_v,
    g_send, g_recv, s_send, s_recv, t_send, t_recv, f_sem, r_sem, loc_sem, own_sem, out_sem,
):
    s_me, f_me = lax.axis_index("src"), lax.axis_index("freq")
    h, z = s_me // Z, lax.rem(s_me, Z)
    targets = {
        "z+": {"src": h * Z + lax.rem(z + 1, Z), "freq": f_me},
        "z-": {"src": h * Z + lax.rem(z + Z - 1, Z), "freq": f_me},
        "y": {"src": (1 - h) * Z + z, "freq": f_me},
    }

    def peer(d):
        return lax.rem(f_me + d, FRQ)

    def rows_of(half, offset):
        hh = h if half == OWN else 1 - h
        block = hh * Z + lax.rem(z + offset + Z, Z)
        return pl.ds(pl.multiple_of(block * ROWS, 16), ROWS)

    def move(k, l, receiving):
        way, half, offset, (lane, width) = MOVES[k]
        if not receiving:
            if way == "y":
                half = 1 - half
            else:
                offset = offset + (1 if way == "z+" else -1)
        ref = gath.at[l, rows_of(half, offset), pl.ds(lane, width)]
        return pltpu.make_async_remote_copy(
            src_ref=ref, dst_ref=ref, send_sem=g_send.at[l, k], recv_sem=g_recv.at[l, k],
            device_id=targets[way], device_id_type=MESH,
        )

    def send(k, l):
        move(k, l, False).start()

    def arrived(k, l):
        move(k, l, True).wait_recv()

    mine = pl.ds(pl.multiple_of(s_me * ROWS, 16), ROWS)

    def focus_copy(part, l):
        return pltpu.make_async_copy(
            focus.at[part, l], gath.at[l, mine, pl.ds(part * NPTS, NPTS)], f_sem.at[part, l]
        )

    def refl_copy(part, l):
        return pltpu.make_async_copy(
            refl.at[part, l], mat.at[l, pl.ds(part * ROWS, ROWS)], r_sem.at[part, l]
        )

    others = [
        pltpu.make_async_copy(a, b, loc_sem.at[i])
        for i, (a, b) in enumerate(((table, tab_v), (onset, on_v), (ending, end_v), (direct, dir_v)))
    ]
    for l in range(L):
        for part in range(2):
            focus_copy(part, l).start()

    barrier = pltpu.get_barrier_semaphore()
    for way in ("z+", "z-", "y"):
        pl.semaphore_signal(barrier, inc=1, device_id=targets[way], device_id_type=MESH)
    for d in range(1, FRQ):
        pl.semaphore_signal(
            barrier, inc=1, device_id={"src": s_me, "freq": peer(d)}, device_id_type=MESH
        )
    for l in range(L):
        for part in range(2):
            refl_copy(part, l).start()
    for c in others:
        c.start()
    for l in range(L):
        for part in range(2):
            focus_copy(part, l).wait()
    pl.semaphore_wait(barrier, 3 + FRQ - 1)

    def phase(body):
        def step(l, carry):
            body(l)
            return carry

        lax.fori_loop(0, L, step, 0)

    def start_own(l):
        send(ZP1, l)
        send(ZM1, l)
        send(Y0, l)

    def near(l):
        arrived(ZP1, l)
        send(ZP2, l)
        send(YM1, l)
        arrived(ZM1, l)
        send(ZM2, l)
        send(YP1, l)

    def second(l):
        arrived(ZP2, l)
        send(ZP3, l)
        arrived(ZM2, l)
        send(ZM3, l)

    def third(l):
        arrived(ZP3, l)
        send(ZP4, l)
        send(YM3, l)
        arrived(ZM3, l)
        send(ZM4, l)
        send(YP3, l)
        arrived(YM1, l)
        send(ZQ2, l)
        arrived(YP1, l)
        send(ZN2, l)

    def fourth(l):
        arrived(ZP4, l)
        arrived(ZM4, l)
        send(Y4, l)
        arrived(ZQ2, l)
        send(ZQ3, l)
        arrived(ZN2, l)
        send(ZN3, l)

    def piece_copy(d, l, receiving):
        to = peer(d)
        place = peer(FRQ - d) if receiving else f_me
        return pltpu.make_async_remote_copy(
            src_ref=spec.at[l, pl.ds(pl.multiple_of(to * PIECE, 8), PIECE)],
            dst_ref=got.at[l, pl.ds(pl.multiple_of(place * PIECE, 8), PIECE)],
            send_sem=s_send.at[l, d], recv_sem=s_recv.at[l, d],
            device_id={"src": s_me, "freq": to}, device_id_type=MESH,
        )

    def own_piece(l):
        rows = pl.ds(pl.multiple_of(f_me * PIECE, 8), PIECE)
        return pltpu.make_async_copy(spec.at[l, rows], got.at[l, rows], own_sem.at[l])

    def product(l):
        for k in (Y0, YM3, YP3, ZQ3, ZN3, Y4):
            arrived(k, l)
        for part in range(2):
            refl_copy(part, l).wait()
        both = jnp.dot(mat[l], gath[l], preferred_element_type=jnp.float32)
        re = both[:ROWS, :NPTS] - both[ROWS:, NPTS:]
        im = both[:ROWS, NPTS:] + both[ROWS:, :NPTS]
        for part, value in enumerate((re, im)):
            for j in range(PER):
                for p in (0, 8):
                    spec[l, pl.ds(p * PIECE + part * PER + j, 8, stride=PIECE), :] = value[
                        16 * j + p : 16 * j + p + 8
                    ]
        own_piece(l).start()
        for d in range(1, FRQ):
            piece_copy(d, l, False).start()

    phase(start_own)
    phase(near)
    phase(second)
    phase(third)
    phase(fourth)
    for c in others:
        c.wait()
    high, low = split(tab_v[...])
    tab3[...] = jnp.concatenate([high, high, low], axis=1)
    phase(product)

    def collect(l):
        own_piece(l).wait()
        for d in range(1, FRQ):
            piece_copy(d, l, True).wait_recv()

    phase(collect)
    for j in range(PER):
        cols = jnp.concatenate(
            [
                got[l, pl.ds(part * PER + j, FRQ, stride=PIECE), :]
                for l in range(L)
                for part in range(2)
            ],
            axis=0,
        )
        high, low = split(cols)
        result = jnp.dot(
            tab3[...],
            jnp.concatenate([high, low, high], axis=0),
            preferred_element_type=jnp.float32,
        )
        for d in range(FRQ):
            trace[pl.ds(d * BACK + j * 8, 8), :] = result[8 * d : 8 * d + 8]

    def back_copy(d, receiving):
        to = peer(d)
        place = peer(FRQ - d) if receiving else f_me
        return pltpu.make_async_remote_copy(
            src_ref=trace.at[pl.ds(pl.multiple_of(to * BACK, 8), BACK)],
            dst_ref=back.at[pl.ds(pl.multiple_of(place * BACK, 8), BACK)],
            send_sem=t_send.at[d], recv_sem=t_recv.at[d],
            device_id={"src": s_me, "freq": to}, device_id_type=MESH,
        )

    rows = pl.ds(pl.multiple_of(f_me * BACK, 8), BACK)
    own_back = pltpu.make_async_copy(trace.at[rows], back.at[rows], own_sem.at[L])
    for d in range(1, FRQ):
        back_copy(d, False).start()
    own_back.start()
    own_back.wait()
    for d in range(1, FRQ):
        back_copy(d, True).wait_recv()

    def out_copy(t):
        return pltpu.make_async_copy(out_v.at[t], out.at[t], out_sem.at[t])

    for t in range(8):
        sample = lax.rem(128 - (8 * f_me + t), 128)
        for j in range(PER):
            for p in (0, 8):
                r = pl.ds(16 * j + p, 8)
                value = back[pl.ds(p * BACK + j * 8 + t, 8, stride=BACK), :]
                window = (sample >= on_v[r, :]) & (sample < end_v[r, :])
                out_v[t, r, :] = dir_v[t, r, :] - jnp.where(window, value, 0.0)
        out_copy(t).start()

    def sent(l):
        for k in range(len(MOVES)):
            move(k, l, False).wait_send()
        for d in range(1, FRQ):
            piece_copy(d, l, False).wait_send()

    phase(sent)
    for d in range(1, FRQ):
        back_copy(d, False).wait_send()
    for t in range(8):
        out_copy(t).wait()


def transform_table():
    device = np.arange(FRQ)
    reverse = sum(((device >> b) & 1) << (3 - b) for b in range(4))
    frequency = (np.arange(L)[:, None] * FRQ + reverse[None, :]).astype(np.int64)
    angle = (np.arange(128)[:, None, None] * frequency[None]) % 128 * (2.0 * np.pi / 128)
    full = np.stack([np.cos(angle), np.sin(angle)], axis=2).reshape(128, 128) / 8.0
    return full.astype(np.float32)


def per_device(reflection, focusing, direct_field, onset_index, end_index):
    f32, bf16 = jnp.float32, jnp.bfloat16
    dma = pltpu.SemaphoreType.DMA
    hbm = pl.BlockSpec(memory_space=pltpu.HBM)
    return pl.pallas_call(
        kernel,
        out_shape=jax.ShapeDtypeStruct((8, ROWS, NPTS), f32),
        in_specs=[hbm] * 6,
        out_specs=hbm,
        scratch_shapes=[
            pltpu.VMEM((L, NSRC, 2 * NPTS), bf16),
            pltpu.VMEM((L, 2 * ROWS, NSRC), bf16),
            pltpu.VMEM((L, FRQ * PIECE, NPTS), f32),
            pltpu.VMEM((L, FRQ * PIECE, NPTS), f32),
            pltpu.VMEM((FRQ * BACK, NPTS), f32),
            pltpu.VMEM((FRQ * BACK, NPTS), f32),
            pltpu.VMEM((8, ROWS, NPTS), f32),
            pltpu.VMEM((ROWS, NPTS), jnp.int32),
            pltpu.VMEM((ROWS, NPTS), jnp.int32),
            pltpu.VMEM((128, 128), f32),
            pltpu.VMEM((128, 384), bf16),
            pltpu.VMEM((8, ROWS, NPTS), f32),
            dma((L, len(MOVES))),
            dma((L, len(MOVES))),
            dma((L, FRQ)),
            dma((L, FRQ)),
            dma((FRQ,)),
            dma((FRQ,)),
            dma((2, L)),
            dma((2, L)),
            dma((4,)),
            dma((L + 1,)),
            dma((8,)),
        ],
        compiler_params=pltpu.CompilerParams(
            collective_id=0, has_side_effects=True, vmem_limit_bytes=63 * 2**20
        ),
        name="marchenko",
    )(
        reflection, focusing, direct_field, onset_index, end_index,
        jnp.asarray(transform_table()),
    )


def solution(mesh):
    placed = (
        P(None, "freq", "src", None),
        P(None, "freq", "src", None),
        P("freq", "src", None),
        P("src", None),
        P("src", None),
    )
    return jax.shard_map(
        per_device, mesh=mesh, in_specs=placed, out_specs=P("freq", "src", None), check_vma=False
    )
```

```python
import functools

import jax
import jax.numpy as jnp
import ml_dtypes
import numpy as np
from jax import lax
from jax.experimental import pallas as pl
from jax.experimental.pallas import tpu as pltpu
from jax.sharding import PartitionSpec as P

MESH = pl.DeviceIdType.MESH

Z = 8
SRC = 16
FRQ = 16
L = 4
ROWS = 144
NPTS = 128
NSRC = SRC * ROWS
PER = ROWS // FRQ
PIECE = 24
LAG = 3
BACK = PER * 8

A, B, ALL = (0, 128), (128, 128), (0, 256)
OWN, PAR = 0, 1
MOVES = (
    ("z+", OWN, -1, ALL),
    ("z+", OWN, -2, ALL),
    ("z+", OWN, -3, ALL),
    ("z+", OWN, -4, A),
    ("z+", PAR, -2, ALL),
    ("z+", PAR, -3, A),
    ("z-", OWN, 1, ALL),
    ("z-", OWN, 2, ALL),
    ("z-", OWN, 3, ALL),
    ("z-", OWN, 4, B),
    ("z-", PAR, 2, ALL),
    ("z-", PAR, 3, A),
    ("y", PAR, 0, ALL),
    ("y", PAR, -1, ALL),
    ("y", PAR, 1, ALL),
    ("y", PAR, -3, B),
    ("y", PAR, 3, B),
    ("y", PAR, 4, ALL),
)
ZP1, ZP2, ZP3, ZP4, ZQ2, ZQ3, ZM1, ZM2, ZM3, ZM4, ZN2, ZN3, Y0, YM1, YP1, YM3, YP3, Y4 = range(18)


def split(value):
    high = value.astype(jnp.bfloat16)
    return high, (value - high.astype(jnp.float32)).astype(jnp.bfloat16)


def kernel(
    refl, focus, direct, onset, ending, table,
    out,
    gath, mat, spec, got, trace, back, dir_v, on_v, end_v, tab_v, tab_a, tab_b, early,
    g_send, g_recv, s_send, s_recv, t_send, t_recv, f_sem, r_sem, loc_sem, own_sem,
):
    s_me, f_me = lax.axis_index("src"), lax.axis_index("freq")
    h, z = s_me // Z, lax.rem(s_me, Z)
    targets = {
        "z+": {"src": h * Z + lax.rem(z + 1, Z), "freq": f_me},
        "z-": {"src": h * Z + lax.rem(z + Z - 1, Z), "freq": f_me},
        "y": {"src": (1 - h) * Z + z, "freq": f_me},
    }

    def peer(d):
        return lax.rem(f_me + d, FRQ)

    def rows_of(half, offset):
        hh = h if half == OWN else 1 - h
        block = hh * Z + lax.rem(z + offset + Z, Z)
        return pl.ds(pl.multiple_of(block * ROWS, 16), ROWS)

    def move(k, l, receiving):
        way, half, offset, (lane, width) = MOVES[k]
        if not receiving:
            if way == "y":
                half = 1 - half
            else:
                offset = offset + (1 if way == "z+" else -1)
        ref = gath.at[l, rows_of(half, offset), pl.ds(lane, width)]
        return pltpu.make_async_remote_copy(
            src_ref=ref, dst_ref=ref, send_sem=g_send.at[l, k], recv_sem=g_recv.at[l, k],
            device_id=targets[way], device_id_type=MESH,
        )

    def send(k, l):
        move(k, l, False).start()

    def arrived(k, l):
        move(k, l, True).wait_recv()

    mine = pl.ds(pl.multiple_of(s_me * ROWS, 16), ROWS)

    def focus_copy(part, l):
        return pltpu.make_async_copy(
            focus.at[part, l], gath.at[l, mine, pl.ds(part * NPTS, NPTS)], f_sem.at[part, l]
        )

    def refl_copy(part, l):
        return pltpu.make_async_copy(
            refl.at[part, l], mat.at[l, pl.ds(part * ROWS, ROWS)], r_sem.at[part, l]
        )

    others = [
        pltpu.make_async_copy(a, b, loc_sem.at[i])
        for i, (a, b) in enumerate(((table, tab_v), (onset, on_v), (ending, end_v), (direct, dir_v)))
    ]
    for l in range(L):
        for part in range(2):
            focus_copy(part, l).start()

    barrier = pltpu.get_barrier_semaphore()
    for way in ("z+", "z-", "y"):
        pl.semaphore_signal(barrier, inc=1, device_id=targets[way], device_id_type=MESH)
    for d in range(1, FRQ):
        pl.semaphore_signal(
            barrier, inc=1, device_id={"src": s_me, "freq": peer(d)}, device_id_type=MESH
        )
    for l in range(L):
        for part in range(2):
            refl_copy(part, l).start()
    for c in others:
        c.start()
    for l in range(L):
        for part in range(2):
            focus_copy(part, l).wait()
    pl.semaphore_wait(barrier, 3 + FRQ - 1)

    def phase(body):
        def step(l, carry):
            body(l)
            return carry

        lax.fori_loop(0, L, step, 0)

    def start_own(l):
        send(ZP1, l)
        send(ZM1, l)
        send(Y0, l)

    def near(l):
        arrived(ZP1, l)
        send(ZP2, l)
        send(YM1, l)
        arrived(ZM1, l)
        send(ZM2, l)
        send(YP1, l)

    def second(l):
        arrived(ZP2, l)
        send(ZP3, l)
        arrived(ZM2, l)
        send(ZM3, l)

    def third(l):
        arrived(ZP3, l)
        send(ZP4, l)
        send(YM3, l)
        arrived(ZM3, l)
        send(ZM4, l)
        send(YP3, l)
        arrived(YM1, l)
        send(ZQ2, l)
        arrived(YP1, l)
        send(ZN2, l)

    def fourth(l):
        arrived(ZP4, l)
        arrived(ZM4, l)
        send(Y4, l)
        arrived(ZQ2, l)
        send(ZQ3, l)
        arrived(ZN2, l)
        send(ZN3, l)

    def piece_copy(d, l, receiving):
        to = peer(d)
        place = peer(FRQ - d) if receiving else f_me
        return pltpu.make_async_remote_copy(
            src_ref=spec.at[l, pl.ds(pl.multiple_of(to * PIECE, 8), 2 * PER)],
            dst_ref=got.at[l, pl.ds(pl.multiple_of(place * PIECE, 8), 2 * PER)],
            send_sem=s_send.at[l, d], recv_sem=s_recv.at[l, d],
            device_id={"src": s_me, "freq": to}, device_id_type=MESH,
        )

    def own_piece(l):
        rows = pl.ds(pl.multiple_of(f_me * PIECE, 8), 2 * PER)
        return pltpu.make_async_copy(spec.at[l, rows], got.at[l, rows], own_sem.at[l])

    def product(l):
        for k in (Y0, YM3, YP3, ZQ3, ZN3, Y4):
            arrived(k, l)
        for part in range(2):
            refl_copy(part, l).wait()
        both = jnp.dot(mat[l], gath[l], preferred_element_type=jnp.float32)
        re = both[:ROWS, :NPTS] - both[ROWS:, NPTS:]
        im = both[:ROWS, NPTS:] + both[ROWS:, :NPTS]
        for part, value in enumerate((re, im)):
            for j in range(PER):
                for p in (0, 8):
                    spec[l, pl.ds(p * PIECE + part * PER + j, 8, stride=PIECE), :] = value[
                        16 * j + p : 16 * j + p + 8
                    ]
        own_piece(l).start()
        for d in range(1, FRQ):
            piece_copy(d, l, False).start()

    phase(start_own)
    phase(near)
    phase(second)
    phase(third)
    for c in others:
        c.wait()
    tab_a[...] = tab_v[:, :384].astype(jnp.bfloat16)
    tab_b[...] = tab_v[:, 384:].astype(jnp.bfloat16)

    def last(i, carry):
        @pl.when(i < L)
        def _():
            fourth(i)

        @pl.when(i >= LAG)
        def _():
            product(i - LAG)

        return carry

    lax.fori_loop(0, L + LAG, last, 0)

    def collect(l):
        own_piece(l).wait()
        for d in range(1, FRQ):
            piece_copy(d, l, True).wait_recv()

    def columns(j, l):
        high, low = split(
            jnp.concatenate(
                [got[l, pl.ds(part * PER + j, FRQ, stride=PIECE), :] for part in range(2)], axis=0
            )
        )
        return jnp.concatenate([high, low, high], axis=0)

    def transform(tab, j, ls):
        js = range(j, min(j + 2, PER))
        cols = jnp.concatenate(
            [jnp.concatenate([columns(k, l) for l in ls], axis=0) for k in js], axis=1
        )
        result = jnp.dot(tab, cols, preferred_element_type=jnp.float32)
        return [(k, result[:, NPTS * i : NPTS * (i + 1)]) for i, k in enumerate(js)]

    for l in range(L - 1):
        collect(l)
    for j in range(0, PER, 2):
        for k, result in transform(tab_a[:, : 96 * (L - 1)], j, range(L - 1)):
            early[k] = result
    collect(L - 1)
    for j in range(0, PER, 2):
        for k, result in transform(tab_b[:, :96], j, (L - 1,)):
            result = result + early[k]
            for d in range(FRQ):
                trace[pl.ds(d * BACK + k * 8, 8), :] = result[8 * d : 8 * d + 8]

    def back_copy(d, receiving):
        to = peer(d)
        place = peer(FRQ - d) if receiving else f_me
        return pltpu.make_async_remote_copy(
            src_ref=trace.at[pl.ds(pl.multiple_of(to * BACK, 8), BACK)],
            dst_ref=back.at[pl.ds(pl.multiple_of(place * BACK, 8), BACK)],
            send_sem=t_send.at[d], recv_sem=t_recv.at[d],
            device_id={"src": s_me, "freq": to}, device_id_type=MESH,
        )

    rows = pl.ds(pl.multiple_of(f_me * BACK, 8), BACK)
    own_back = pltpu.make_async_copy(trace.at[rows], back.at[rows], own_sem.at[L])
    for d in range(1, FRQ):
        back_copy(d, False).start()
    own_back.start()
    own_back.wait()
    for d in range(1, FRQ):
        back_copy(d, True).wait_recv()

    for t in range(8):
        sample = lax.rem(128 - (8 * f_me + t), 128)
        for j in range(PER):
            for p in (0, 8):
                r = pl.ds(16 * j + p, 8)
                value = back[pl.ds(p * BACK + j * 8 + t, 8, stride=BACK), :]
                window = (sample >= on_v[r, :]) & (sample < end_v[r, :])
                out[t, r, :] = dir_v[t, r, :] - jnp.where(window, value, 0.0)

    def sent(l):
        for k in range(len(MOVES)):
            move(k, l, False).wait_send()
        for d in range(1, FRQ):
            piece_copy(d, l, False).wait_send()

    phase(sent)
    for d in range(1, FRQ):
        back_copy(d, False).wait_send()


def transform_table():
    device = np.arange(FRQ)
    reverse = sum(((device >> b) & 1) << (3 - b) for b in range(4))
    frequency = (np.arange(L)[:, None] * FRQ + reverse[None, :]).astype(np.int64)
    angle = (np.arange(128)[:, None, None] * frequency[None]) % 128 * (2.0 * np.pi / 128)
    full = np.stack([np.cos(angle), np.sin(angle)], axis=2).reshape(128, L, 32) / 8.0
    full = full.astype(np.float32)
    high = full.astype(ml_dtypes.bfloat16).astype(np.float32)
    low = (full - high).astype(ml_dtypes.bfloat16).astype(np.float32)
    three = np.concatenate([high, high, low], axis=2)
    table = np.zeros((128, 512), np.float32)
    table[:, : 96 * (L - 1)] = three[:, : L - 1].reshape(128, 96 * (L - 1))
    table[:, 384:480] = three[:, L - 1]
    return table


def per_device(reflection, focusing, direct_field, onset_index, end_index):
    f32, bf16 = jnp.float32, jnp.bfloat16
    dma = pltpu.SemaphoreType.DMA
    hbm = pl.BlockSpec(memory_space=pltpu.HBM)
    return pl.pallas_call(
        kernel,
        out_shape=pltpu.VMEM((8, ROWS, NPTS), f32),
        in_specs=[hbm] * 6,
        out_specs=pl.BlockSpec(memory_space=pltpu.VMEM),
        scratch_shapes=[
            pltpu.VMEM((L, NSRC, 2 * NPTS), bf16),
            pltpu.VMEM((L, 2 * ROWS, NSRC), bf16),
            pltpu.VMEM((L, FRQ * PIECE, NPTS), f32),
            pltpu.VMEM((L, FRQ * PIECE, NPTS), f32),
            pltpu.VMEM((FRQ * BACK, NPTS), f32),
            pltpu.VMEM((FRQ * BACK, NPTS), f32),
            pltpu.VMEM((8, ROWS, NPTS), f32),
            pltpu.VMEM((ROWS, NPTS), jnp.int32),
            pltpu.VMEM((ROWS, NPTS), jnp.int32),
            pltpu.VMEM((128, 512), f32),
            pltpu.VMEM((128, 384), bf16),
            pltpu.VMEM((128, 128), bf16),
            pltpu.VMEM((PER, 128, NPTS), f32),
            dma((L, len(MOVES))),
            dma((L, len(MOVES))),
            dma((L, FRQ)),
            dma((L, FRQ)),
            dma((FRQ,)),
            dma((FRQ,)),
            dma((2, L)),
            dma((2, L)),
            dma((4,)),
            dma((L + 1,)),
        ],
        compiler_params=pltpu.CompilerParams(
            collective_id=0, has_side_effects=True, vmem_limit_bytes=60 * 2**20
        ),
        name="marchenko",
    )(
        reflection, focusing, direct_field, onset_index, end_index,
        jnp.asarray(transform_table()),
    )


def solution(mesh):
    placed = (
        P(None, "freq", "src", None),
        P(None, "freq", "src", None),
        P("freq", "src", None),
        P("src", None),
        P("src", None),
    )
    return jax.shard_map(
        per_device, mesh=mesh, in_specs=placed, out_specs=P("freq", "src", None), check_vma=False
    )
```

```python
import functools

import jax
import jax.numpy as jnp
import ml_dtypes
import numpy as np
from jax import lax
from jax.experimental import pallas as pl
from jax.experimental.pallas import tpu as pltpu
from jax.sharding import PartitionSpec as P

MESH = pl.DeviceIdType.MESH

Z = 8
SRC = 16
FRQ = 16
L = 4
ROWS = 144
NPTS = 128
NSRC = SRC * ROWS
PER = ROWS // FRQ
PIECE = 24
USED = PER + 1
LAG = 3
BACK = (PER + 1) // 2 * 8

A, B, ALL = (0, 128), (128, 128), (0, 256)
OWN, PAR = 0, 1
MOVES = (
    ("z+", OWN, -1, ALL),
    ("z+", OWN, -2, ALL),
    ("z+", OWN, -3, ALL),
    ("z+", OWN, -4, A),
    ("z+", PAR, -2, ALL),
    ("z+", PAR, -3, A),
    ("z-", OWN, 1, ALL),
    ("z-", OWN, 2, ALL),
    ("z-", OWN, 3, ALL),
    ("z-", OWN, 4, B),
    ("z-", PAR, 2, ALL),
    ("z-", PAR, 3, A),
    ("y", PAR, 0, ALL),
    ("y", PAR, -1, ALL),
    ("y", PAR, 1, ALL),
    ("y", PAR, -3, B),
    ("y", PAR, 3, B),
    ("y", PAR, 4, ALL),
)
ZP1, ZP2, ZP3, ZP4, ZQ2, ZQ3, ZM1, ZM2, ZM3, ZM4, ZN2, ZN3, Y0, YM1, YP1, YM3, YP3, Y4 = range(18)


def split(value):
    high = value.astype(jnp.bfloat16)
    return high, (value - high.astype(jnp.float32)).astype(jnp.bfloat16)


def block_scale(largest):
    code = jnp.ceil(jnp.log2(jnp.maximum(largest, 2.0**-126)) * 16.0)
    half = jnp.exp2(code * (-1.0 / 32))
    return code.astype(jnp.int32), half, half * 32700.0


def scale_of(code):
    half = jnp.exp2(code.astype(jnp.float32) * (1.0 / 32))
    return half, half * (1.0 / 32700)


def to_int(value, scale):
    return jnp.floor(value * scale[0] * scale[1] + 0.5).astype(jnp.int32)


def pack(first, second):
    return (first << 16) | (second & 0xFFFF)


def first_of(word):
    return word >> 16


def second_of(word):
    return (word << 16) >> 16


def kernel(
    refl, focus, direct, onset, ending, table,
    out,
    gath, mat, spec, got, trace, back, dir_v, on_v, end_v, tab_v, tab_a, tab_b, early,
    g_send, g_recv, s_send, s_recv, t_send, t_recv, f_sem, r_sem, loc_sem, own_sem,
):
    s_me, f_me = lax.axis_index("src"), lax.axis_index("freq")
    h, z = s_me // Z, lax.rem(s_me, Z)
    targets = {
        "z+": {"src": h * Z + lax.rem(z + 1, Z), "freq": f_me},
        "z-": {"src": h * Z + lax.rem(z + Z - 1, Z), "freq": f_me},
        "y": {"src": (1 - h) * Z + z, "freq": f_me},
    }

    def peer(d):
        return lax.rem(f_me + d, FRQ)

    def rows_of(half, offset):
        hh = h if half == OWN else 1 - h
        block = hh * Z + lax.rem(z + offset + Z, Z)
        return pl.ds(pl.multiple_of(block * ROWS, 16), ROWS)

    def move(k, l, receiving):
        way, half, offset, (lane, width) = MOVES[k]
        if not receiving:
            if way == "y":
                half = 1 - half
            else:
                offset = offset + (1 if way == "z+" else -1)
        ref = gath.at[l, rows_of(half, offset), pl.ds(lane, width)]
        return pltpu.make_async_remote_copy(
            src_ref=ref, dst_ref=ref, send_sem=g_send.at[l, k], recv_sem=g_recv.at[l, k],
            device_id=targets[way], device_id_type=MESH,
        )

    def send(k, l):
        move(k, l, False).start()

    def arrived(k, l):
        move(k, l, True).wait_recv()

    mine = pl.ds(pl.multiple_of(s_me * ROWS, 16), ROWS)

    def focus_copy(part, l):
        return pltpu.make_async_copy(
            focus.at[part, l], gath.at[l, mine, pl.ds(part * NPTS, NPTS)], f_sem.at[part, l]
        )

    def refl_copy(part, l):
        return pltpu.make_async_copy(
            refl.at[part, l], mat.at[l, pl.ds(part * ROWS, ROWS)], r_sem.at[part, l]
        )

    others = [
        pltpu.make_async_copy(a, b, loc_sem.at[i])
        for i, (a, b) in enumerate(((table, tab_v), (onset, on_v), (ending, end_v), (direct, dir_v)))
    ]
    for l in range(L):
        for part in range(2):
            focus_copy(part, l).start()

    barrier = pltpu.get_barrier_semaphore()
    for way in ("z+", "z-", "y"):
        pl.semaphore_signal(barrier, inc=1, device_id=targets[way], device_id_type=MESH)
    for d in range(1, FRQ):
        pl.semaphore_signal(
            barrier, inc=1, device_id={"src": s_me, "freq": peer(d)}, device_id_type=MESH
        )
    for l in range(L):
        for part in range(2):
            refl_copy(part, l).start()
    for c in others:
        c.start()
    for l in range(L):
        for part in range(2):
            focus_copy(part, l).wait()
    pl.semaphore_wait(barrier, 3 + FRQ - 1)

    def phase(body):
        def step(l, carry):
            body(l)
            return carry

        lax.fori_loop(0, L, step, 0)

    def start_own(l):
        send(ZP1, l)
        send(ZM1, l)
        send(Y0, l)

    def near(l):
        arrived(ZP1, l)
        send(ZP2, l)
        send(YM1, l)
        arrived(ZM1, l)
        send(ZM2, l)
        send(YP1, l)

    def second(l):
        arrived(ZP2, l)
        send(ZP3, l)
        arrived(ZM2, l)
        send(ZM3, l)

    def third(l):
        arrived(ZP3, l)
        send(ZP4, l)
        send(YM3, l)
        arrived(ZM3, l)
        send(ZM4, l)
        send(YP3, l)
        arrived(YM1, l)
        send(ZQ2, l)
        arrived(YP1, l)
        send(ZN2, l)

    def fourth(l):
        arrived(ZP4, l)
        arrived(ZM4, l)
        send(Y4, l)
        arrived(ZQ2, l)
        send(ZQ3, l)
        arrived(ZN2, l)
        send(ZN3, l)

    def piece_copy(d, l, receiving):
        to = peer(d)
        place = peer(FRQ - d) if receiving else f_me
        return pltpu.make_async_remote_copy(
            src_ref=spec.at[l, pl.ds(pl.multiple_of(to * PIECE, 8), USED)],
            dst_ref=got.at[l, pl.ds(pl.multiple_of(place * PIECE, 8), USED)],
            send_sem=s_send.at[l, d], recv_sem=s_recv.at[l, d],
            device_id={"src": s_me, "freq": to}, device_id_type=MESH,
        )

    def own_piece(l):
        rows = pl.ds(pl.multiple_of(f_me * PIECE, 8), USED)
        return pltpu.make_async_copy(spec.at[l, rows], got.at[l, rows], own_sem.at[l])

    def product(l):
        for k in (Y0, YM3, YP3, ZQ3, ZN3, Y4):
            arrived(k, l)
        for part in range(2):
            refl_copy(part, l).wait()
        both = jnp.dot(mat[l], gath[l], preferred_element_type=jnp.float32)
        re = both[:ROWS, :NPTS] - both[ROWS:, NPTS:]
        im = both[:ROWS, NPTS:] + both[ROWS:, :NPTS]
        for p in (0, 8):
            rows = [slice(16 * j + p, 16 * j + p + 8) for j in range(PER)]
            largest = functools.reduce(
                jnp.maximum, [jnp.maximum(jnp.abs(re[r]), jnp.abs(im[r])) for r in rows]
            )
            code, *scale = block_scale(largest)
            words = [pack(to_int(re[r], scale), to_int(im[r], scale)) for r in rows]
            for j, word in enumerate(words + [code]):
                spec[l, pl.ds(p * PIECE + j, 8, stride=PIECE), :] = word
        own_piece(l).start()
        for d in range(1, FRQ):
            piece_copy(d, l, False).start()

    phase(start_own)
    phase(near)
    phase(second)
    phase(third)
    for c in others:
        c.wait()
    tab_a[...] = tab_v[:, :384].astype(jnp.bfloat16)
    tab_b[...] = tab_v[:, 384:].astype(jnp.bfloat16)

    def last(i, carry):
        @pl.when(i < L)
        def _():
            fourth(i)

        @pl.when(i >= LAG)
        def _():
            product(i - LAG)

        return carry

    lax.fori_loop(0, L + LAG, last, 0)

    def collect(l):
        own_piece(l).wait()
        for d in range(1, FRQ):
            piece_copy(d, l, True).wait_recv()

    def columns(j, l):
        word = got[l, pl.ds(j, FRQ, stride=PIECE), :]
        one, two = scale_of(got[l, pl.ds(PER, FRQ, stride=PIECE), :])
        high, low = split(
            jnp.concatenate(
                [part(word).astype(jnp.float32) * one * two for part in (first_of, second_of)], axis=0
            )
        )
        return jnp.concatenate([high, low, high], axis=0)

    def transform(tab, j, ls):
        js = range(j, min(j + 2, PER))
        cols = jnp.concatenate(
            [jnp.concatenate([columns(k, l) for l in ls], axis=0) for k in js], axis=1
        )
        result = jnp.dot(tab, cols, preferred_element_type=jnp.float32)
        return [(k, result[:, NPTS * i : NPTS * (i + 1)]) for i, k in enumerate(js)]

    for l in range(L - 1):
        collect(l)
    for j in range(0, PER, 2):
        for k, result in transform(tab_a[:, : 96 * (L - 1)], j, range(L - 1)):
            early[k] = result
    sample = lax.rem(128 - lax.broadcasted_iota(jnp.int32, (128, NPTS), 0), 128)
    collect(L - 1)
    largest = jnp.zeros((128, NPTS), jnp.float32)
    for j in range(0, PER, 2):
        for k, result in transform(tab_b[:, :96], j, (L - 1,)):
            r = pl.ds(16 * k + f_me, 1)
            window = (sample >= on_v[r, :]) & (sample < end_v[r, :])
            result = jnp.where(window, result + early[k], 0.0)
            early[k] = result
            largest = jnp.maximum(largest, jnp.abs(result))
    code, *scale = block_scale(largest)
    for j in range(0, PER, 2):
        word = pack(
            to_int(early[j], scale), to_int(early[j + 1], scale) if j + 1 < PER else code
        )
        for d in range(FRQ):
            trace[pl.ds(d * BACK + j * 4, 8), :] = word[8 * d : 8 * d + 8]

    def back_copy(d, receiving):
        to = peer(d)
        place = peer(FRQ - d) if receiving else f_me
        return pltpu.make_async_remote_copy(
            src_ref=trace.at[pl.ds(pl.multiple_of(to * BACK, 8), BACK)],
            dst_ref=back.at[pl.ds(pl.multiple_of(place * BACK, 8), BACK)],
            send_sem=t_send.at[d], recv_sem=t_recv.at[d],
            device_id={"src": s_me, "freq": to}, device_id_type=MESH,
        )

    rows = pl.ds(pl.multiple_of(f_me * BACK, 8), BACK)
    own_back = pltpu.make_async_copy(trace.at[rows], back.at[rows], own_sem.at[L])
    for d in range(1, FRQ):
        back_copy(d, False).start()
    own_back.start()
    own_back.wait()
    for d in range(1, FRQ):
        back_copy(d, True).wait_recv()

    for t in range(8):
        for p in (0, 8):
            words = [
                back[pl.ds(p * BACK + i * 8 + t, 8, stride=BACK), :] for i in range((PER + 1) // 2)
            ]
            one, two = scale_of(second_of(words[-1]))
            for j in range(PER):
                value = (first_of, second_of)[j % 2](words[j // 2]).astype(jnp.float32)
                r = pl.ds(16 * j + p, 8)
                out[t, r, :] = dir_v[t, r, :] - value * one * two

    def sent(l):
        for k in range(len(MOVES)):
            move(k, l, False).wait_send()
        for d in range(1, FRQ):
            piece_copy(d, l, False).wait_send()

    phase(sent)
    for d in range(1, FRQ):
        back_copy(d, False).wait_send()


def transform_table():
    device = np.arange(FRQ)
    reverse = sum(((device >> b) & 1) << (3 - b) for b in range(4))
    frequency = (np.arange(L)[:, None] * FRQ + reverse[None, :]).astype(np.int64)
    angle = (np.arange(128)[:, None, None] * frequency[None]) % 128 * (2.0 * np.pi / 128)
    full = np.stack([np.cos(angle), np.sin(angle)], axis=2).reshape(128, L, 32) / 8.0
    full = full.astype(np.float32)
    high = full.astype(ml_dtypes.bfloat16).astype(np.float32)
    low = (full - high).astype(ml_dtypes.bfloat16).astype(np.float32)
    three = np.concatenate([high, high, low], axis=2)
    table = np.zeros((128, 512), np.float32)
    table[:, : 96 * (L - 1)] = three[:, : L - 1].reshape(128, 96 * (L - 1))
    table[:, 384:480] = three[:, L - 1]
    return table


def per_device(reflection, focusing, direct_field, onset_index, end_index):
    f32, bf16 = jnp.float32, jnp.bfloat16
    dma = pltpu.SemaphoreType.DMA
    hbm = pl.BlockSpec(memory_space=pltpu.HBM)
    return pl.pallas_call(
        kernel,
        out_shape=pltpu.VMEM((8, ROWS, NPTS), f32),
        in_specs=[hbm] * 6,
        out_specs=pl.BlockSpec(memory_space=pltpu.VMEM),
        scratch_shapes=[
            pltpu.VMEM((L, NSRC, 2 * NPTS), bf16),
            pltpu.VMEM((L, 2 * ROWS, NSRC), bf16),
            pltpu.VMEM((L, FRQ * PIECE, NPTS), jnp.int32),
            pltpu.VMEM((L, FRQ * PIECE, NPTS), jnp.int32),
            pltpu.VMEM((FRQ * BACK, NPTS), jnp.int32),
            pltpu.VMEM((FRQ * BACK, NPTS), jnp.int32),
            pltpu.VMEM((8, ROWS, NPTS), f32),
            pltpu.VMEM((ROWS, NPTS), jnp.int32),
            pltpu.VMEM((ROWS, NPTS), jnp.int32),
            pltpu.VMEM((128, 512), f32),
            pltpu.VMEM((128, 384), bf16),
            pltpu.VMEM((128, 128), bf16),
            pltpu.VMEM((PER, 128, NPTS), f32),
            dma((L, len(MOVES))),
            dma((L, len(MOVES))),
            dma((L, FRQ)),
            dma((L, FRQ)),
            dma((FRQ,)),
            dma((FRQ,)),
            dma((2, L)),
            dma((2, L)),
            dma((4,)),
            dma((L + 1,)),
        ],
        compiler_params=pltpu.CompilerParams(
            collective_id=0, has_side_effects=True, vmem_limit_bytes=60 * 2**20
        ),
        name="marchenko",
    )(
        reflection, focusing, direct_field, onset_index, end_index,
        jnp.asarray(transform_table()),
    )


def solution(mesh):
    placed = (
        P(None, "freq", "src", None),
        P(None, "freq", "src", None),
        P("freq", "src", None),
        P("src", None),
        P("src", None),
    )
    return jax.shard_map(
        per_device, mesh=mesh, in_specs=placed, out_specs=P("freq", "src", None), check_vma=False
    )
```

```python
import functools

import jax
import jax.numpy as jnp
import ml_dtypes
import numpy as np
from jax import lax
from jax.experimental import pallas as pl
from jax.experimental.pallas import tpu as pltpu
from jax.sharding import PartitionSpec as P

MESH = pl.DeviceIdType.MESH

Z = 8
SRC = 16
FRQ = 16
L = 4
ROWS = 144
NPTS = 128
NSRC = SRC * ROWS
PER = ROWS // FRQ
PIECE = 24
USED = PER + 1
LAG = 3
BACK = (PER + 1) // 2 * 8

PEERS = (10, 11, 8, 9, 6, 14, 7, 15, 4, 12, 5, 13, 2, 3, 1)
A, B, ALL = (0, 128), (128, 128), (0, 256)
OWN, PAR = 0, 1
MOVES = (
    ("z+", OWN, -1, ALL, 0),
    ("z+", OWN, -2, ALL, 1),
    ("z+", OWN, -3, ALL, 2),
    ("z+", OWN, -4, A, 3),
    ("z+", PAR, -2, ALL, 5),
    ("z+", PAR, -3, A, 6),
    ("z-", OWN, 1, ALL, 0),
    ("z-", OWN, 2, ALL, 1),
    ("z-", OWN, 3, ALL, 2),
    ("z-", OWN, 4, B, 3),
    ("z-", PAR, 2, ALL, 5),
    ("z-", PAR, 3, A, 6),
    ("y", PAR, 0, ALL, 6),
    ("y", PAR, -1, ALL, 4),
    ("y", PAR, 1, ALL, 4),
    ("y", PAR, -3, B, 6),
    ("y", PAR, 3, B, 6),
    ("y", PAR, 4, ALL, 6),
)
ZP1, ZP2, ZP3, ZP4, ZQ2, ZQ3, ZM1, ZM2, ZM3, ZM4, ZN2, ZN3, Y0, YM1, YP1, YM3, YP3, Y4 = range(18)
OWN1, OWN2, OWN3, OWN4, PAR1, PAR2, REST = range(7)
BLOCKS = (2, 2, 2, 1, 2, 2, 4)
SENT = sum(BLOCKS)


def split(value):
    high = value.astype(jnp.bfloat16)
    return high, (value - high.astype(jnp.float32)).astype(jnp.bfloat16)


def block_scale(largest):
    code = jnp.ceil(jnp.log2(jnp.maximum(largest, 2.0**-126)) * 16.0)
    half = jnp.exp2(code * (-1.0 / 32))
    return code.astype(jnp.int32), half, half * 32700.0


def scale_of(code):
    half = jnp.exp2(code.astype(jnp.float32) * (1.0 / 32))
    return half, half * (1.0 / 32700)


def to_int(value, scale):
    return jnp.floor(value * scale[0] * scale[1] + 0.5).astype(jnp.int32)


def pack(first, second):
    return (first << 16) | (second & 0xFFFF)


def first_of(word):
    return word >> 16


def second_of(word):
    return (word << 16) >> 16


def kernel(
    refl, focus, direct, onset, ending, table,
    out,
    gath, mat, spec, got, trace, back, dir_v, on_v, end_v, tab_v, tab_a, tab_b, early,
    g_send, g_recv, s_send, s_recv, t_send, t_recv, f_sem, r_sem, loc_sem,
):
    s_me, f_me = lax.axis_index("src"), lax.axis_index("freq")
    h, z = s_me // Z, lax.rem(s_me, Z)
    targets = {
        "z+": {"src": h * Z + lax.rem(z + 1, Z), "freq": f_me},
        "z-": {"src": h * Z + lax.rem(z + Z - 1, Z), "freq": f_me},
        "y": {"src": (1 - h) * Z + z, "freq": f_me},
    }

    x_me, y_me, c_me = f_me // 4, lax.rem(f_me // 2, 2), lax.rem(f_me, 2)

    def peer_at(d):
        dx, dy, dc = d // 4, d // 2 % 2, d % 2
        x = lax.rem(x_me + dx, 4)
        return (x * 2 + lax.rem(y_me + dy, 2)) * 2 + lax.rem(c_me + dc, 2)

    peers = {d: peer_at(d) for d in PEERS}

    def peer(d):
        return peers[d]

    def rows_of(half, offset):
        hh = h if half == OWN else 1 - h
        block = hh * Z + lax.rem(z + offset + Z, Z)
        return pl.ds(pl.multiple_of(block * ROWS, 16), ROWS)

    def send(k, l):
        way, half, offset, (lane, width), group = MOVES[k]
        if way == "y":
            half = 1 - half
        else:
            offset = offset + (1 if way == "z+" else -1)
        ref = gath.at[l, rows_of(half, offset), pl.ds(lane, width)]
        pltpu.make_async_remote_copy(
            src_ref=ref, dst_ref=ref, send_sem=g_send.at[l], recv_sem=g_recv.at[l, group],
            device_id=targets[way], device_id_type=MESH,
        ).start()

    def await_all(ref, sem):
        pltpu.make_async_copy(ref, ref, sem).wait()

    def arrived(group, l):
        await_all(gath.at[l, pl.ds(0, BLOCKS[group] * ROWS)], g_recv.at[l, group])

    mine = pl.ds(pl.multiple_of(s_me * ROWS, 16), ROWS)

    def focus_copy(part, l):
        return pltpu.make_async_copy(
            focus.at[part, l], gath.at[l, mine, pl.ds(part * NPTS, NPTS)], f_sem
        )

    def refl_copy(part, l):
        return pltpu.make_async_copy(
            refl.at[part, l], mat.at[l, pl.ds(part * ROWS, ROWS)], r_sem.at[l]
        )

    others = [
        pltpu.make_async_copy(a, b, loc_sem.at[i])
        for i, (a, b) in enumerate(((table, tab_v), (onset, on_v), (ending, end_v), (direct, dir_v)))
    ]
    barrier = pltpu.get_barrier_semaphore()
    for d in PEERS:
        pl.semaphore_signal(
            barrier, inc=1, device_id={"src": s_me, "freq": peer(d)}, device_id_type=MESH
        )
    for way in ("y", "z+", "z-"):
        pl.semaphore_signal(barrier, inc=1, device_id=targets[way], device_id_type=MESH)
    for l in range(L):
        for part in range(2):
            focus_copy(part, l).start()
    for l in range(L):
        for part in range(2):
            refl_copy(part, l).start()
    for c in others:
        c.start()
    await_all(gath.at[0, pl.ds(0, L * ROWS)], f_sem)
    pl.semaphore_wait(barrier, 3 + FRQ - 1)

    def phase(body):
        def step(l, carry):
            body(l)
            return carry

        lax.fori_loop(0, L, step, 0)

    def start_own(l):
        send(ZP1, l)
        send(ZM1, l)
        send(Y0, l)

    def near(l):
        arrived(OWN1, l)
        for k in (ZP2, ZM2, YM1, YP1):
            send(k, l)

    def second(l):
        arrived(OWN2, l)
        for k in (ZP3, ZM3):
            send(k, l)

    def third(l):
        arrived(OWN3, l)
        for k in (ZP4, ZM4, YM3, YP3):
            send(k, l)
        arrived(PAR1, l)
        for k in (ZQ2, ZN2):
            send(k, l)

    def fourth(l):
        arrived(OWN4, l)
        send(Y4, l)
        arrived(PAR2, l)
        for k in (ZQ3, ZN3):
            send(k, l)

    def piece_copy(d, l):
        return pltpu.make_async_remote_copy(
            src_ref=spec.at[l, pl.ds(pl.multiple_of(peer(d) * PIECE, 8), USED)],
            dst_ref=got.at[l, pl.ds(pl.multiple_of(f_me * PIECE, 8), USED)],
            send_sem=s_send.at[l], recv_sem=s_recv.at[l],
            device_id={"src": s_me, "freq": peer(d)}, device_id_type=MESH,
        )

    def own_piece(l):
        rows = pl.ds(pl.multiple_of(f_me * PIECE, 8), USED)
        return pltpu.make_async_copy(spec.at[l, rows], got.at[l, rows], s_recv.at[l])

    def product(l):
        arrived(REST, l)
        await_all(mat.at[l], r_sem.at[l])
        both = jnp.dot(mat[l], gath[l], preferred_element_type=jnp.float32)
        re = both[:ROWS, :NPTS] - both[ROWS:, NPTS:]
        im = both[:ROWS, NPTS:] + both[ROWS:, :NPTS]
        for p in (0, 8):
            rows = [slice(16 * j + p, 16 * j + p + 8) for j in range(PER)]
            largest = functools.reduce(
                jnp.maximum, [jnp.maximum(jnp.abs(re[r]), jnp.abs(im[r])) for r in rows]
            )
            code, *scale = block_scale(largest)
            words = [pack(to_int(re[r], scale), to_int(im[r], scale)) for r in rows]
            for j, word in enumerate(words + [code]):
                spec[l, pl.ds(p * PIECE + j, 8, stride=PIECE), :] = word
        own_piece(l).start()
        for d in PEERS:
            piece_copy(d, l).start()

    phase(start_own)
    phase(near)
    phase(second)
    phase(third)
    for c in others:
        c.wait()
    tab_a[...] = tab_v[:, :384].astype(jnp.bfloat16)
    tab_b[...] = tab_v[:, 384:].astype(jnp.bfloat16)

    def last(i, carry):
        @pl.when(i < L)
        def _():
            fourth(i)

        @pl.when(i >= LAG)
        def _():
            product(i - LAG)

        return carry

    lax.fori_loop(0, L + LAG, last, 0)

    def collect(l):
        await_all(got.at[l, pl.ds(0, FRQ * USED)], s_recv.at[l])

    def columns(j, l):
        word = got[l, pl.ds(j, FRQ, stride=PIECE), :]
        one, two = scale_of(got[l, pl.ds(PER, FRQ, stride=PIECE), :])
        high, low = split(
            jnp.concatenate(
                [part(word).astype(jnp.float32) * one * two for part in (first_of, second_of)], axis=0
            )
        )
        return jnp.concatenate([high, low, high], axis=0)

    def transform(tab, j, ls):
        js = range(j, min(j + 2, PER))
        cols = jnp.concatenate(
            [jnp.concatenate([columns(k, l) for l in ls], axis=0) for k in js], axis=1
        )
        result = jnp.dot(tab, cols, preferred_element_type=jnp.float32)
        return [(k, result[:, NPTS * i : NPTS * (i + 1)]) for i, k in enumerate(js)]

    for l in range(L - 1):
        collect(l)
    for j in range(0, PER, 2):
        for k, result in transform(tab_a[:, : 96 * (L - 1)], j, range(L - 1)):
            early[k] = result
    sample = lax.rem(128 - lax.broadcasted_iota(jnp.int32, (128, NPTS), 0), 128)
    collect(L - 1)
    largest = jnp.zeros((128, NPTS), jnp.float32)
    for j in range(0, PER, 2):
        for k, result in transform(tab_b[:, :96], j, (L - 1,)):
            r = pl.ds(16 * k + f_me, 1)
            window = (sample >= on_v[r, :]) & (sample < end_v[r, :])
            result = jnp.where(window, result + early[k], 0.0)
            early[k] = result
            largest = jnp.maximum(largest, jnp.abs(result))
    code, *scale = block_scale(largest)
    for j in range(0, PER, 2):
        word = pack(
            to_int(early[j], scale), to_int(early[j + 1], scale) if j + 1 < PER else code
        )
        for d in range(FRQ):
            trace[pl.ds(d * BACK + j * 4, 8), :] = word[8 * d : 8 * d + 8]

    rows = pl.ds(pl.multiple_of(f_me * BACK, 8), BACK)
    for d in PEERS:
        pltpu.make_async_remote_copy(
            src_ref=trace.at[pl.ds(pl.multiple_of(peer(d) * BACK, 8), BACK)],
            dst_ref=back.at[rows],
            send_sem=t_send, recv_sem=t_recv,
            device_id={"src": s_me, "freq": peer(d)}, device_id_type=MESH,
        ).start()
    pltpu.make_async_copy(trace.at[rows], back.at[rows], t_recv).start()
    await_all(back, t_recv)

    for t in range(8):
        for p in (0, 8):
            words = [
                back[pl.ds(p * BACK + i * 8 + t, 8, stride=BACK), :] for i in range((PER + 1) // 2)
            ]
            one, two = scale_of(second_of(words[-1]))
            for j in range(PER):
                value = (first_of, second_of)[j % 2](words[j // 2]).astype(jnp.float32)
                r = pl.ds(16 * j + p, 8)
                out[t, r, :] = dir_v[t, r, :] - value * one * two

    def sent(l):
        await_all(gath.at[l, pl.ds(0, SENT * ROWS)], g_send.at[l])
        await_all(spec.at[l, pl.ds(0, (FRQ - 1) * USED)], s_send.at[l])

    phase(sent)
    await_all(trace.at[pl.ds(0, (FRQ - 1) * BACK)], t_send)


def transform_table():
    device = np.arange(FRQ)
    reverse = sum(((device >> b) & 1) << (3 - b) for b in range(4))
    frequency = (np.arange(L)[:, None] * FRQ + reverse[None, :]).astype(np.int64)
    angle = (np.arange(128)[:, None, None] * frequency[None]) % 128 * (2.0 * np.pi / 128)
    full = np.stack([np.cos(angle), np.sin(angle)], axis=2).reshape(128, L, 32) / 8.0
    full = full.astype(np.float32)
    high = full.astype(ml_dtypes.bfloat16).astype(np.float32)
    low = (full - high).astype(ml_dtypes.bfloat16).astype(np.float32)
    three = np.concatenate([high, high, low], axis=2)
    table = np.zeros((128, 512), np.float32)
    table[:, : 96 * (L - 1)] = three[:, : L - 1].reshape(128, 96 * (L - 1))
    table[:, 384:480] = three[:, L - 1]
    return table


def per_device(reflection, focusing, direct_field, onset_index, end_index):
    f32, bf16 = jnp.float32, jnp.bfloat16
    dma = pltpu.SemaphoreType.DMA
    hbm = pl.BlockSpec(memory_space=pltpu.HBM)
    return pl.pallas_call(
        kernel,
        out_shape=pltpu.VMEM((8, ROWS, NPTS), f32),
        in_specs=[hbm] * 6,
        out_specs=pl.BlockSpec(memory_space=pltpu.VMEM),
        scratch_shapes=[
            pltpu.VMEM((L, NSRC, 2 * NPTS), bf16),
            pltpu.VMEM((L, 2 * ROWS, NSRC), bf16),
            pltpu.VMEM((L, FRQ * PIECE, NPTS), jnp.int32),
            pltpu.VMEM((L, FRQ * PIECE, NPTS), jnp.int32),
            pltpu.VMEM((FRQ * BACK, NPTS), jnp.int32),
            pltpu.VMEM((FRQ * BACK, NPTS), jnp.int32),
            pltpu.VMEM((8, ROWS, NPTS), f32),
            pltpu.VMEM((ROWS, NPTS), jnp.int32),
            pltpu.VMEM((ROWS, NPTS), jnp.int32),
            pltpu.VMEM((128, 512), f32),
            pltpu.VMEM((128, 384), bf16),
            pltpu.VMEM((128, 128), bf16),
            pltpu.VMEM((PER, 128, NPTS), f32),
            dma((L,)),
            dma((L, len(BLOCKS))),
            dma((L,)),
            dma((L,)),
            dma,
            dma,
            dma,
            dma((L,)),
            dma((4,)),
        ],
        compiler_params=pltpu.CompilerParams(
            collective_id=0, has_side_effects=True, vmem_limit_bytes=60 * 2**20
        ),
        name="marchenko",
    )(
        reflection, focusing, direct_field, onset_index, end_index,
        jnp.asarray(transform_table()),
    )


def solution(mesh):
    placed = (
        P(None, "freq", "src", None),
        P(None, "freq", "src", None),
        P("freq", "src", None),
        P("src", None),
        P("src", None),
    )
    return jax.shard_map(
        per_device, mesh=mesh, in_specs=placed, out_specs=P("freq", "src", None), check_vma=False
    )
```

```python
import functools

import jax
import jax.numpy as jnp
import ml_dtypes
import numpy as np
from jax import lax
from jax.experimental import pallas as pl
from jax.experimental.pallas import tpu as pltpu
from jax.sharding import PartitionSpec as P

MESH = pl.DeviceIdType.MESH

Z = 8
SRC = 16
FRQ = 16
L = 4
ROWS = 144
NPTS = 128
NSRC = SRC * ROWS
PER = ROWS // FRQ
PIECE = 24
USED = PER + 1
LAG = 3
BACK = (PER + 1) // 2 * 8

PEERS = (10, 11, 8, 9, 6, 14, 7, 15, 4, 12, 5, 13, 2, 3, 1)
A, B, ALL = (0, 128), (128, 128), (0, 256)
OWN, PAR = 0, 1
MOVES = (
    ("z+", OWN, -1, ALL, 0),
    ("z+", OWN, -2, ALL, 1),
    ("z+", OWN, -3, ALL, 2),
    ("z+", OWN, -4, A, 3),
    ("z+", PAR, -2, ALL, 5),
    ("z+", PAR, -3, A, 6),
    ("z-", OWN, 1, ALL, 0),
    ("z-", OWN, 2, ALL, 1),
    ("z-", OWN, 3, ALL, 2),
    ("z-", OWN, 4, B, 3),
    ("z-", PAR, 2, ALL, 5),
    ("z-", PAR, 3, A, 6),
    ("y", PAR, 0, ALL, 6),
    ("y", PAR, -1, ALL, 4),
    ("y", PAR, 1, ALL, 4),
    ("y", PAR, -3, B, 6),
    ("y", PAR, 3, B, 6),
    ("y", PAR, 4, ALL, 6),
)
ZP1, ZP2, ZP3, ZP4, ZQ2, ZQ3, ZM1, ZM2, ZM3, ZM4, ZN2, ZN3, Y0, YM1, YP1, YM3, YP3, Y4 = range(18)
OWN1, OWN2, OWN3, OWN4, PAR1, PAR2, REST = range(7)
BLOCKS = (2, 2, 2, 1, 2, 2, 4)
SENT = sum(BLOCKS)


def split(value):
    high = value.astype(jnp.bfloat16)
    return high, (value - high.astype(jnp.float32)).astype(jnp.bfloat16)


def block_scale(largest):
    code = jnp.ceil(jnp.log2(jnp.maximum(largest, 2.0**-126)) * 16.0)
    half = jnp.exp2(code * (-1.0 / 32))
    return code.astype(jnp.int32), half, half * 32700.0


def scale_of(code):
    half = jnp.exp2(code.astype(jnp.float32) * (1.0 / 32))
    return half, half * (1.0 / 32700)


def to_int(value, scale):
    return jnp.floor(value * scale[0] * scale[1] + 0.5).astype(jnp.int32)


def pack(first, second):
    return (first << 16) | (second & 0xFFFF)


def first_of(word):
    return word >> 16


def second_of(word):
    return (word << 16) >> 16


def kernel(
    refl, focus, direct, onset, ending, table,
    out,
    gath, mat, spec, got, trace, back, dir_v, on_v, end_v, tab_v, tab_a, tab_b, early,
    g_send, g_recv, s_send, s_recv, t_send, t_recv, f_sem, r_sem, loc_sem,
):
    s_me, f_me = lax.axis_index("src"), lax.axis_index("freq")
    h, z = s_me // Z, lax.rem(s_me, Z)
    targets = {
        "z+": {"src": h * Z + lax.rem(z + 1, Z), "freq": f_me},
        "z-": {"src": h * Z + lax.rem(z + Z - 1, Z), "freq": f_me},
        "y": {"src": (1 - h) * Z + z, "freq": f_me},
    }

    x_me, y_me, c_me = f_me // 4, lax.rem(f_me // 2, 2), lax.rem(f_me, 2)

    def peer_at(d):
        dx, dy, dc = d // 4, d // 2 % 2, d % 2
        x = lax.rem(x_me + dx, 4)
        return (x * 2 + lax.rem(y_me + dy, 2)) * 2 + lax.rem(c_me + dc, 2)

    peers = {d: peer_at(d) for d in PEERS}

    def peer(d):
        return peers[d]

    def rows_of(half, offset):
        hh = h if half == OWN else 1 - h
        block = hh * Z + lax.rem(z + offset + Z, Z)
        return pl.ds(pl.multiple_of(block * ROWS, 16), ROWS)

    def send(k, l):
        way, half, offset, (lane, width), group = MOVES[k]
        if way == "y":
            half = 1 - half
        else:
            offset = offset + (1 if way == "z+" else -1)
        ref = gath.at[l, rows_of(half, offset), pl.ds(lane, width)]
        pltpu.make_async_remote_copy(
            src_ref=ref, dst_ref=ref, send_sem=g_send, recv_sem=g_recv.at[l, group],
            device_id=targets[way], device_id_type=MESH,
        ).start()

    def await_all(ref, sem):
        pltpu.make_async_copy(ref, ref, sem).wait()

    def arrived(group, l):
        await_all(gath.at[l, pl.ds(0, BLOCKS[group] * ROWS)], g_recv.at[l, group])

    mine = pl.ds(pl.multiple_of(s_me * ROWS, 16), ROWS)

    def focus_copy(part, l):
        return pltpu.make_async_copy(
            focus.at[part, l], gath.at[l, mine, pl.ds(part * NPTS, NPTS)], f_sem
        )

    def refl_copy(part, l):
        return pltpu.make_async_copy(
            refl.at[part, l], mat.at[l, pl.ds(part * ROWS, ROWS)], r_sem
        )

    others = [
        pltpu.make_async_copy(a, b, loc_sem.at[i])
        for i, (a, b) in enumerate(((table, tab_v), (onset, on_v), (ending, end_v), (direct, dir_v)))
    ]
    barrier = pltpu.get_barrier_semaphore()
    for d in PEERS:
        pl.semaphore_signal(
            barrier, inc=1, device_id={"src": s_me, "freq": peer(d)}, device_id_type=MESH
        )
    for way in ("y", "z+", "z-"):
        pl.semaphore_signal(barrier, inc=1, device_id=targets[way], device_id_type=MESH)
    for l in range(L):
        for part in range(2):
            focus_copy(part, l).start()
    for l in range(L):
        for part in range(2):
            refl_copy(part, l).start()
    for c in others:
        c.start()
    await_all(gath.at[0, pl.ds(0, L * ROWS)], f_sem)
    pl.semaphore_wait(barrier, 3 + FRQ - 1)

    def phase(body):
        def step(l, carry):
            body(l)
            return carry

        lax.fori_loop(0, L, step, 0)

    def start_own(l):
        send(ZP1, l)
        send(ZM1, l)
        send(Y0, l)

    def near(l):
        arrived(OWN1, l)
        for k in (ZP2, ZM2, YM1, YP1):
            send(k, l)

    def second(l):
        arrived(OWN2, l)
        for k in (ZP3, ZM3):
            send(k, l)

    def third(l):
        arrived(OWN3, l)
        for k in (ZP4, ZM4, YM3, YP3):
            send(k, l)
        arrived(PAR1, l)
        for k in (ZQ2, ZN2):
            send(k, l)

    def fourth(l):
        arrived(OWN4, l)
        send(Y4, l)
        arrived(PAR2, l)
        for k in (ZQ3, ZN3):
            send(k, l)

    def piece_copy(d, l):
        return pltpu.make_async_remote_copy(
            src_ref=spec.at[l, pl.ds(pl.multiple_of(peer(d) * PIECE, 8), USED)],
            dst_ref=got.at[l, pl.ds(pl.multiple_of(f_me * PIECE, 8), USED)],
            send_sem=s_send, recv_sem=s_recv.at[l],
            device_id={"src": s_me, "freq": peer(d)}, device_id_type=MESH,
        )

    def own_piece(l):
        rows = pl.ds(pl.multiple_of(f_me * PIECE, 8), USED)
        return pltpu.make_async_copy(spec.at[l, rows], got.at[l, rows], s_recv.at[l])

    def product(l):
        arrived(REST, l)
        both = jnp.dot(mat[l], gath[l], preferred_element_type=jnp.float32)
        re = both[:ROWS, :NPTS] - both[ROWS:, NPTS:]
        im = both[:ROWS, NPTS:] + both[ROWS:, :NPTS]
        for p in (0, 8):
            rows = [slice(16 * j + p, 16 * j + p + 8) for j in range(PER)]
            largest = functools.reduce(
                jnp.maximum, [jnp.maximum(jnp.abs(re[r]), jnp.abs(im[r])) for r in rows]
            )
            code, *scale = block_scale(largest)
            words = [pack(to_int(re[r], scale), to_int(im[r], scale)) for r in rows]
            for j, word in enumerate(words + [code]):
                spec[l, pl.ds(p * PIECE + j, 8, stride=PIECE), :] = word
        own_piece(l).start()
        for d in PEERS:
            piece_copy(d, l).start()

    phase(start_own)
    phase(near)
    phase(second)
    phase(third)
    await_all(mat, r_sem)
    for c in others:
        c.wait()
    tab_a[...] = tab_v[:, :384].astype(jnp.bfloat16)
    tab_b[...] = tab_v[:, 384:].astype(jnp.bfloat16)

    def last(i, carry):
        @pl.when(i < L)
        def _():
            fourth(i)

        @pl.when(i >= LAG)
        def _():
            product(i - LAG)

        return carry

    lax.fori_loop(0, L + LAG, last, 0)

    def collect(l):
        await_all(got.at[l, pl.ds(0, FRQ * USED)], s_recv.at[l])

    def columns(j, l):
        word = got[l, pl.ds(j, FRQ, stride=PIECE), :]
        one, two = scale_of(got[l, pl.ds(PER, FRQ, stride=PIECE), :])
        high, low = split(
            jnp.concatenate(
                [part(word).astype(jnp.float32) * one * two for part in (first_of, second_of)], axis=0
            )
        )
        return jnp.concatenate([high, low, high], axis=0)

    def transform(tab, j, ls):
        js = range(j, min(j + 2, PER))
        cols = jnp.concatenate(
            [jnp.concatenate([columns(k, l) for l in ls], axis=0) for k in js], axis=1
        )
        result = jnp.dot(tab, cols, preferred_element_type=jnp.float32)
        return [(k, result[:, NPTS * i : NPTS * (i + 1)]) for i, k in enumerate(js)]

    for l in range(L - 1):
        collect(l)
    for j in range(0, PER, 2):
        for k, result in transform(tab_a[:, : 96 * (L - 1)], j, range(L - 1)):
            early[k] = result
    sample = lax.rem(128 - lax.broadcasted_iota(jnp.int32, (128, NPTS), 0), 128)
    collect(L - 1)
    largest = jnp.zeros((128, NPTS), jnp.float32)
    for j in range(0, PER, 2):
        for k, result in transform(tab_b[:, :96], j, (L - 1,)):
            r = pl.ds(16 * k + f_me, 1)
            window = (sample >= on_v[r, :]) & (sample < end_v[r, :])
            result = jnp.where(window, result + early[k], 0.0)
            early[k] = result
            largest = jnp.maximum(largest, jnp.abs(result))
    code, *scale = block_scale(largest)
    for j in range(0, PER, 2):
        word = pack(
            to_int(early[j], scale), to_int(early[j + 1], scale) if j + 1 < PER else code
        )
        for d in range(FRQ):
            trace[pl.ds(d * BACK + j * 4, 8), :] = word[8 * d : 8 * d + 8]

    rows = pl.ds(pl.multiple_of(f_me * BACK, 8), BACK)
    for d in PEERS:
        pltpu.make_async_remote_copy(
            src_ref=trace.at[pl.ds(pl.multiple_of(peer(d) * BACK, 8), BACK)],
            dst_ref=back.at[rows],
            send_sem=t_send, recv_sem=t_recv,
            device_id={"src": s_me, "freq": peer(d)}, device_id_type=MESH,
        ).start()
    pltpu.make_async_copy(trace.at[rows], back.at[rows], t_recv).start()
    await_all(back.at[pl.ds(0, FRQ * BACK)], t_recv)

    for t in range(8):
        for p in (0, 8):
            words = [
                back[pl.ds(p * BACK + i * 8 + t, 8, stride=BACK), :] for i in range((PER + 1) // 2)
            ]
            one, two = scale_of(second_of(words[-1]))
            for j in range(PER):
                value = (first_of, second_of)[j % 2](words[j // 2]).astype(jnp.float32)
                r = pl.ds(16 * j + p, 8)
                out[t, r, :] = dir_v[t, r, :] - value * one * two

    await_all(gath.at[:, pl.ds(0, SENT * ROWS)], g_send)
    await_all(spec.at[:, pl.ds(0, (FRQ - 1) * USED)], s_send)
    await_all(trace.at[pl.ds(0, (FRQ - 1) * BACK)], t_send)


def transform_table():
    device = np.arange(FRQ)
    reverse = sum(((device >> b) & 1) << (3 - b) for b in range(4))
    frequency = (np.arange(L)[:, None] * FRQ + reverse[None, :]).astype(np.int64)
    angle = (np.arange(128)[:, None, None] * frequency[None]) % 128 * (2.0 * np.pi / 128)
    full = np.stack([np.cos(angle), np.sin(angle)], axis=2).reshape(128, L, 32) / 8.0
    full = full.astype(np.float32)
    high = full.astype(ml_dtypes.bfloat16).astype(np.float32)
    low = (full - high).astype(ml_dtypes.bfloat16).astype(np.float32)
    three = np.concatenate([high, high, low], axis=2)
    table = np.zeros((128, 512), np.float32)
    table[:, : 96 * (L - 1)] = three[:, : L - 1].reshape(128, 96 * (L - 1))
    table[:, 384:480] = three[:, L - 1]
    return table


def per_device(reflection, focusing, direct_field, onset_index, end_index):
    f32, bf16 = jnp.float32, jnp.bfloat16
    dma = pltpu.SemaphoreType.DMA
    hbm = pl.BlockSpec(memory_space=pltpu.HBM)
    return pl.pallas_call(
        kernel,
        out_shape=pltpu.VMEM((8, ROWS, NPTS), f32),
        in_specs=[hbm] * 6,
        out_specs=pl.BlockSpec(memory_space=pltpu.VMEM),
        scratch_shapes=[
            pltpu.VMEM((L, NSRC, 2 * NPTS), bf16),
            pltpu.VMEM((L, 2 * ROWS, NSRC), bf16),
            pltpu.VMEM((L, (FRQ + 1) * PIECE, NPTS), jnp.int32),
            pltpu.VMEM((L, (FRQ + 1) * PIECE, NPTS), jnp.int32),
            pltpu.VMEM(((FRQ + 1) * BACK, NPTS), jnp.int32),
            pltpu.VMEM(((FRQ + 1) * BACK, NPTS), jnp.int32),
            pltpu.VMEM((8, ROWS, NPTS), f32),
            pltpu.VMEM((ROWS, NPTS), jnp.int32),
            pltpu.VMEM((ROWS, NPTS), jnp.int32),
            pltpu.VMEM((128, 512), f32),
            pltpu.VMEM((128, 384), bf16),
            pltpu.VMEM((128, 128), bf16),
            pltpu.VMEM((PER, 128, NPTS), f32),
            dma,
            dma((L, len(BLOCKS))),
            dma,
            dma((L,)),
            dma,
            dma,
            dma,
            dma,
            dma((4,)),
        ],
        compiler_params=pltpu.CompilerParams(
            collective_id=0, has_side_effects=True, vmem_limit_bytes=60 * 2**20
        ),
        name="marchenko",
    )(
        reflection, focusing, direct_field, onset_index, end_index,
        jnp.asarray(transform_table()),
    )


def solution(mesh):
    placed = (
        P(None, "freq", "src", None),
        P(None, "freq", "src", None),
        P("freq", "src", None),
        P("src", None),
        P("src", None),
    )
    return jax.shard_map(
        per_device, mesh=mesh, in_specs=placed, out_specs=P("freq", "src", None), check_vma=False
    )
```

```python
import functools

import jax
import jax.numpy as jnp
import ml_dtypes
import numpy as np
from jax import lax
from jax.experimental import pallas as pl
from jax.experimental.pallas import tpu as pltpu
from jax.sharding import PartitionSpec as P

MESH = pl.DeviceIdType.MESH

Z = 8
SRC = 16
FRQ = 16
L = 4
ROWS = 144
NPTS = 128
NSRC = SRC * ROWS
PER = ROWS // FRQ
PIECE = 24
USED = PER + 1
LAG = 3
BACK = (PER + 1) // 2 * 8

PEERS = (10, 6, 14, 11, 7, 15, 8, 4, 12, 9, 5, 13, 2, 3, 1)
A, B, ALL = (0, 128), (128, 128), (0, 256)
OWN, PAR = 0, 1
MOVES = (
    ("z+", OWN, -1, ALL, 0),
    ("z+", OWN, -2, ALL, 1),
    ("z+", OWN, -3, ALL, 2),
    ("z+", OWN, -4, A, 3),
    ("z+", PAR, -2, ALL, 5),
    ("z+", PAR, -3, A, 6),
    ("z-", OWN, 1, ALL, 0),
    ("z-", OWN, 2, ALL, 1),
    ("z-", OWN, 3, ALL, 2),
    ("z-", OWN, 4, B, 3),
    ("z-", PAR, 2, ALL, 5),
    ("z-", PAR, 3, A, 6),
    ("y", PAR, 0, ALL, 6),
    ("y", PAR, -1, ALL, 4),
    ("y", PAR, 1, ALL, 4),
    ("y", PAR, -3, B, 6),
    ("y", PAR, 3, B, 6),
    ("y", PAR, 4, ALL, 6),
)
ZP1, ZP2, ZP3, ZP4, ZQ2, ZQ3, ZM1, ZM2, ZM3, ZM4, ZN2, ZN3, Y0, YM1, YP1, YM3, YP3, Y4 = range(18)
OWN1, OWN2, OWN3, OWN4, PAR1, PAR2, REST = range(7)
BLOCKS = (2, 2, 2, 1, 2, 2, 4)
SENT = sum(BLOCKS)


def split(value):
    high = value.astype(jnp.bfloat16)
    return high, (value - high.astype(jnp.float32)).astype(jnp.bfloat16)


def block_scale(largest):
    code = jnp.ceil(jnp.log2(jnp.maximum(largest, 2.0**-126)) * 16.0)
    half = jnp.exp2(code * (-1.0 / 32))
    return code.astype(jnp.int32), half, half * 32700.0


def scale_of(code):
    half = jnp.exp2(code.astype(jnp.float32) * (1.0 / 32))
    return half, half * (1.0 / 32700)


def to_int(value, scale):
    return jnp.floor(value * scale[0] * scale[1] + 0.5).astype(jnp.int32)


def pack(first, second):
    return (first << 16) | (second & 0xFFFF)


def first_of(word):
    return word >> 16


def second_of(word):
    return (word << 16) >> 16


def kernel(
    refl, focus, direct, onset, ending, table,
    out,
    gath, mat, spec, got, trace, back, dir_v, on_v, end_v, tab_v, tab_a, tab_b, early,
    g_send, g_recv, s_send, s_recv, t_send, t_recv, f_sem, r_sem, loc_sem,
):
    s_me, f_me = lax.axis_index("src"), lax.axis_index("freq")
    h, z = s_me // Z, lax.rem(s_me, Z)
    targets = {
        "z+": {"src": h * Z + lax.rem(z + 1, Z), "freq": f_me},
        "z-": {"src": h * Z + lax.rem(z + Z - 1, Z), "freq": f_me},
        "y": {"src": (1 - h) * Z + z, "freq": f_me},
    }

    x_me, y_me, c_me = f_me // 4, lax.rem(f_me // 2, 2), lax.rem(f_me, 2)

    def peer_at(d):
        dx, dy, dc = d // 4, d // 2 % 2, d % 2
        x = lax.rem(x_me + dx, 4)
        return (x * 2 + lax.rem(y_me + dy, 2)) * 2 + lax.rem(c_me + dc, 2)

    peers = {d: peer_at(d) for d in PEERS}

    def peer(d):
        return peers[d]

    def rows_of(half, offset):
        hh = h if half == OWN else 1 - h
        block = hh * Z + lax.rem(z + offset + Z, Z)
        return pl.ds(pl.multiple_of(block * ROWS, 16), ROWS)

    def send(k, l):
        way, half, offset, (lane, width), group = MOVES[k]
        if way == "y":
            half = 1 - half
        else:
            offset = offset + (1 if way == "z+" else -1)
        ref = gath.at[l, rows_of(half, offset), pl.ds(lane, width)]
        pltpu.make_async_remote_copy(
            src_ref=ref, dst_ref=ref, send_sem=g_send, recv_sem=g_recv.at[l, group],
            device_id=targets[way], device_id_type=MESH,
        ).start()

    def await_all(ref, sem):
        pltpu.make_async_copy(ref, ref, sem).wait()

    def arrived(group, l):
        await_all(gath.at[l, pl.ds(0, BLOCKS[group] * ROWS)], g_recv.at[l, group])

    mine = pl.ds(pl.multiple_of(s_me * ROWS, 16), ROWS)

    def focus_copy(part, l):
        return pltpu.make_async_copy(
            focus.at[part, l], gath.at[l, mine, pl.ds(part * NPTS, NPTS)], f_sem
        )

    def refl_copy(part, l):
        return pltpu.make_async_copy(
            refl.at[part, l], mat.at[l, pl.ds(part * ROWS, ROWS)], r_sem
        )

    others = [
        pltpu.make_async_copy(a, b, loc_sem.at[i])
        for i, (a, b) in enumerate(((table, tab_v), (onset, on_v), (ending, end_v), (direct, dir_v)))
    ]
    barrier = pltpu.get_barrier_semaphore()
    for d in PEERS:
        pl.semaphore_signal(
            barrier, inc=1, device_id={"src": s_me, "freq": peer(d)}, device_id_type=MESH
        )
    for way in ("y", "z+", "z-"):
        pl.semaphore_signal(barrier, inc=1, device_id=targets[way], device_id_type=MESH)
    for l in range(L):
        for part in range(2):
            focus_copy(part, l).start()
    for l in range(L):
        for part in range(2):
            refl_copy(part, l).start()
    for c in others:
        c.start()
    await_all(gath.at[0, pl.ds(0, L * ROWS)], f_sem)
    pl.semaphore_wait(barrier, 3 + FRQ - 1)

    def phase(body):
        def step(l, carry):
            body(l)
            return carry

        lax.fori_loop(0, L, step, 0)

    def start_own(l):
        send(ZP1, l)
        send(ZM1, l)
        send(Y0, l)

    def near(l):
        arrived(OWN1, l)
        for k in (ZP2, ZM2, YM1, YP1):
            send(k, l)

    def second(l):
        arrived(OWN2, l)
        for k in (ZP3, ZM3):
            send(k, l)

    def third(l):
        arrived(OWN3, l)
        for k in (ZP4, ZM4, YM3, YP3):
            send(k, l)
        arrived(PAR1, l)
        for k in (ZQ2, ZN2):
            send(k, l)

    def fourth(l):
        arrived(OWN4, l)
        send(Y4, l)
        arrived(PAR2, l)
        for k in (ZQ3, ZN3):
            send(k, l)

    def piece_copy(d, l):
        return pltpu.make_async_remote_copy(
            src_ref=spec.at[l, pl.ds(pl.multiple_of(peer(d) * PIECE, 8), USED)],
            dst_ref=got.at[l, pl.ds(pl.multiple_of(f_me * PIECE, 8), USED)],
            send_sem=s_send, recv_sem=s_recv.at[l],
            device_id={"src": s_me, "freq": peer(d)}, device_id_type=MESH,
        )

    def own_piece(l):
        rows = pl.ds(pl.multiple_of(f_me * PIECE, 8), USED)
        return pltpu.make_async_copy(spec.at[l, rows], got.at[l, rows], s_recv.at[l])

    def product(l):
        arrived(REST, l)
        both = jnp.dot(mat[l], gath[l], preferred_element_type=jnp.float32)
        re = both[:ROWS, :NPTS] - both[ROWS:, NPTS:]
        im = both[:ROWS, NPTS:] + both[ROWS:, :NPTS]
        for p in (0, 8):
            rows = [slice(16 * j + p, 16 * j + p + 8) for j in range(PER)]
            largest = functools.reduce(
                jnp.maximum, [jnp.maximum(jnp.abs(re[r]), jnp.abs(im[r])) for r in rows]
            )
            code, *scale = block_scale(largest)
            words = [pack(to_int(re[r], scale), to_int(im[r], scale)) for r in rows]
            for j, word in enumerate(words + [code]):
                spec[l, pl.ds(p * PIECE + j, 8, stride=PIECE), :] = word
        own_piece(l).start()
        for d in PEERS:
            piece_copy(d, l).start()

    phase(start_own)
    phase(near)
    phase(second)
    phase(third)
    await_all(mat, r_sem)
    for c in others:
        c.wait()
    tab_a[...] = tab_v[:, :384].astype(jnp.bfloat16)
    tab_b[...] = tab_v[:, 384:].astype(jnp.bfloat16)

    def last(i, carry):
        @pl.when(i < L)
        def _():
            fourth(i)

        @pl.when(i >= LAG)
        def _():
            product(i - LAG)

        return carry

    lax.fori_loop(0, L + LAG, last, 0)

    def collect(l):
        await_all(got.at[l, pl.ds(0, FRQ * USED)], s_recv.at[l])

    def columns(j, l):
        word = got[l, pl.ds(j, FRQ, stride=PIECE), :]
        one, two = scale_of(got[l, pl.ds(PER, FRQ, stride=PIECE), :])
        high, low = split(
            jnp.concatenate(
                [part(word).astype(jnp.float32) * one * two for part in (first_of, second_of)], axis=0
            )
        )
        return jnp.concatenate([high, low, high], axis=0)

    def transform(tab, j, ls):
        js = range(j, min(j + 2, PER))
        cols = jnp.concatenate(
            [jnp.concatenate([columns(k, l) for l in ls], axis=0) for k in js], axis=1
        )
        result = jnp.dot(tab, cols, preferred_element_type=jnp.float32)
        return [(k, result[:, NPTS * i : NPTS * (i + 1)]) for i, k in enumerate(js)]

    for l in range(L - 1):
        collect(l)
    for j in range(0, PER, 2):
        for k, result in transform(tab_a[:, : 96 * (L - 1)], j, range(L - 1)):
            early[k] = result
    sample = lax.rem(128 - lax.broadcasted_iota(jnp.int32, (128, NPTS), 0), 128)
    collect(L - 1)
    largest = jnp.zeros((128, NPTS), jnp.float32)
    for j in range(0, PER, 2):
        for k, result in transform(tab_b[:, :96], j, (L - 1,)):
            r = pl.ds(16 * k + f_me, 1)
            window = (sample >= on_v[r, :]) & (sample < end_v[r, :])
            result = jnp.where(window, result + early[k], 0.0)
            early[k] = result
            largest = jnp.maximum(largest, jnp.abs(result))
    code, *scale = block_scale(largest)
    for j in range(0, PER, 2):
        word = pack(
            to_int(early[j], scale), to_int(early[j + 1], scale) if j + 1 < PER else code
        )
        for d in range(FRQ):
            trace[pl.ds(d * BACK + j * 4, 8), :] = word[8 * d : 8 * d + 8]

    rows = pl.ds(pl.multiple_of(f_me * BACK, 8), BACK)
    for d in PEERS:
        pltpu.make_async_remote_copy(
            src_ref=trace.at[pl.ds(pl.multiple_of(peer(d) * BACK, 8), BACK)],
            dst_ref=back.at[rows],
            send_sem=t_send, recv_sem=t_recv,
            device_id={"src": s_me, "freq": peer(d)}, device_id_type=MESH,
        ).start()
    pltpu.make_async_copy(trace.at[rows], back.at[rows], t_recv).start()
    await_all(back.at[pl.ds(0, FRQ * BACK)], t_recv)

    for t in range(8):
        for p in (0, 8):
            words = [
                back[pl.ds(p * BACK + i * 8 + t, 8, stride=BACK), :] for i in range((PER + 1) // 2)
            ]
            one, two = scale_of(second_of(words[-1]))
            for j in range(PER):
                value = (first_of, second_of)[j % 2](words[j // 2]).astype(jnp.float32)
                r = pl.ds(16 * j + p, 8)
                out[t, r, :] = dir_v[t, r, :] - value * one * two

    await_all(gath.at[:, pl.ds(0, SENT * ROWS)], g_send)
    await_all(spec.at[:, pl.ds(0, (FRQ - 1) * USED)], s_send)
    await_all(trace.at[pl.ds(0, (FRQ - 1) * BACK)], t_send)


def transform_table():
    device = np.arange(FRQ)
    reverse = sum(((device >> b) & 1) << (3 - b) for b in range(4))
    frequency = (np.arange(L)[:, None] * FRQ + reverse[None, :]).astype(np.int64)
    angle = (np.arange(128)[:, None, None] * frequency[None]) % 128 * (2.0 * np.pi / 128)
    full = np.stack([np.cos(angle), np.sin(angle)], axis=2).reshape(128, L, 32) / 8.0
    full = full.astype(np.float32)
    high = full.astype(ml_dtypes.bfloat16).astype(np.float32)
    low = (full - high).astype(ml_dtypes.bfloat16).astype(np.float32)
    three = np.concatenate([high, high, low], axis=2)
    table = np.zeros((128, 512), np.float32)
    table[:, : 96 * (L - 1)] = three[:, : L - 1].reshape(128, 96 * (L - 1))
    table[:, 384:480] = three[:, L - 1]
    return table


def per_device(reflection, focusing, direct_field, onset_index, end_index):
    f32, bf16 = jnp.float32, jnp.bfloat16
    dma = pltpu.SemaphoreType.DMA
    hbm = pl.BlockSpec(memory_space=pltpu.HBM)
    return pl.pallas_call(
        kernel,
        out_shape=pltpu.VMEM((8, ROWS, NPTS), f32),
        in_specs=[hbm] * 6,
        out_specs=pl.BlockSpec(memory_space=pltpu.VMEM),
        scratch_shapes=[
            pltpu.VMEM((L, NSRC, 2 * NPTS), bf16),
            pltpu.VMEM((L, 2 * ROWS, NSRC), bf16),
            pltpu.VMEM((L, (FRQ + 1) * PIECE, NPTS), jnp.int32),
            pltpu.VMEM((L, (FRQ + 1) * PIECE, NPTS), jnp.int32),
            pltpu.VMEM(((FRQ + 1) * BACK, NPTS), jnp.int32),
            pltpu.VMEM(((FRQ + 1) * BACK, NPTS), jnp.int32),
            pltpu.VMEM((8, ROWS, NPTS), f32),
            pltpu.VMEM((ROWS, NPTS), jnp.int32),
            pltpu.VMEM((ROWS, NPTS), jnp.int32),
            pltpu.VMEM((128, 512), f32),
            pltpu.VMEM((128, 384), bf16),
            pltpu.VMEM((128, 128), bf16),
            pltpu.VMEM((PER, 128, NPTS), f32),
            dma,
            dma((L, len(BLOCKS))),
            dma,
            dma((L,)),
            dma,
            dma,
            dma,
            dma,
            dma((4,)),
        ],
        compiler_params=pltpu.CompilerParams(
            collective_id=0, has_side_effects=True, vmem_limit_bytes=60 * 2**20
        ),
        name="marchenko",
    )(
        reflection, focusing, direct_field, onset_index, end_index,
        jnp.asarray(transform_table()),
    )


def solution(mesh):
    placed = (
        P(None, "freq", "src", None),
        P(None, "freq", "src", None),
        P("freq", "src", None),
        P("src", None),
        P("src", None),
    )
    return jax.shard_map(
        per_device, mesh=mesh, in_specs=placed, out_specs=P("freq", "src", None), check_vma=False
    )
```

```python
import functools

import jax
import jax.numpy as jnp
import ml_dtypes
import numpy as np
from jax import lax
from jax.experimental import pallas as pl
from jax.experimental.pallas import tpu as pltpu
from jax.sharding import PartitionSpec as P

MESH = pl.DeviceIdType.MESH

Z = 8
SRC = 16
FRQ = 16
L = 4
ROWS = 144
NPTS = 128
NSRC = SRC * ROWS
PER = ROWS // FRQ
PIECE = 24
USED = PER + 1
LAG = 4
BACK = (PER + 1) // 2 * 8

PEERS = (10, 6, 14, 11, 7, 15, 8, 4, 12, 9, 5, 13, 2, 3, 1)
A, B, ALL = (0, 144, 0, 128), (0, 144, 128, 128), (0, 144, 0, 256)
TOP, LOW = (0, 80, 0, 256), (80, 64, 0, 256)
OWN, PAR = 0, 1
MOVES = (
    ("z+", OWN, -1, ALL, 0),
    ("z+", OWN, -2, ALL, 1),
    ("z+", OWN, -3, ALL, 2),
    ("z+", OWN, -4, A, 3),
    ("z+", PAR, -2, ALL, 5),
    ("z+", PAR, -3, TOP, 6),
    ("z-", OWN, 1, ALL, 0),
    ("z-", OWN, 2, ALL, 1),
    ("z-", OWN, 3, ALL, 2),
    ("z-", OWN, 4, B, 3),
    ("z-", PAR, 2, ALL, 5),
    ("z-", PAR, 3, TOP, 6),
    ("y", PAR, 0, ALL, 6),
    ("y", PAR, -1, ALL, 4),
    ("y", PAR, 1, ALL, 4),
    ("y", PAR, -3, LOW, 6),
    ("y", PAR, 3, LOW, 6),
    ("y", PAR, 4, ALL, 6),
)
ZP1, ZP2, ZP3, ZP4, ZQ2, ZQ3, ZM1, ZM2, ZM3, ZM4, ZN2, ZN3, Y0, YM1, YP1, YM3, YP3, Y4 = range(18)
OWN1, OWN2, OWN3, OWN4, PAR1, PAR2, REST = range(7)
BLOCKS = (2, 2, 2, 1, 2, 2, 4)
SENT = sum(BLOCKS)


def split(value):
    high = value.astype(jnp.bfloat16)
    return high, (value - high.astype(jnp.float32)).astype(jnp.bfloat16)


def block_scale(largest):
    code = jnp.ceil(jnp.log2(jnp.maximum(largest, 2.0**-126)) * 16.0)
    half = jnp.exp2(code * (-1.0 / 32))
    return code.astype(jnp.int32), half, half * 32700.0


def scale_of(code):
    half = jnp.exp2(code.astype(jnp.float32) * (1.0 / 32))
    return half, half * (1.0 / 32700)


def to_int(value, scale):
    return jnp.floor(value * scale[0] * scale[1] + 0.5).astype(jnp.int32)


def pack(first, second):
    return (first << 16) | (second & 0xFFFF)


def first_of(word):
    return word >> 16


def second_of(word):
    return (word << 16) >> 16


def kernel(
    refl, focus, direct, onset, ending, table,
    out,
    gath, mat, spec, got, trace, back, dir_v, on_v, end_v, tab_v, tab_a, tab_b, early,
    g_send, g_recv, s_send, s_recv, t_send, t_recv, f_sem, r_sem, loc_sem,
):
    s_me, f_me = lax.axis_index("src"), lax.axis_index("freq")
    h, z = s_me // Z, lax.rem(s_me, Z)
    targets = {
        "z+": {"src": h * Z + lax.rem(z + 1, Z), "freq": f_me},
        "z-": {"src": h * Z + lax.rem(z + Z - 1, Z), "freq": f_me},
        "y": {"src": (1 - h) * Z + z, "freq": f_me},
    }

    x_me, y_me, c_me = f_me // 4, lax.rem(f_me // 2, 2), lax.rem(f_me, 2)

    def peer_at(d):
        dx, dy, dc = d // 4, d // 2 % 2, d % 2
        x = lax.rem(x_me + dx, 4)
        return (x * 2 + lax.rem(y_me + dy, 2)) * 2 + lax.rem(c_me + dc, 2)

    peers = {d: peer_at(d) for d in PEERS}

    def peer(d):
        return peers[d]

    def rows_of(half, offset, first, count):
        hh = h if half == OWN else 1 - h
        block = hh * Z + lax.rem(z + offset + Z, Z)
        return pl.ds(pl.multiple_of(block * ROWS + first, 16), count)

    def send(k, l):
        way, half, offset, (first, count, lane, width), group = MOVES[k]
        if way == "y":
            half = 1 - half
        else:
            offset = offset + (1 if way == "z+" else -1)
        ref = gath.at[l, rows_of(half, offset, first, count), pl.ds(lane, width)]
        pltpu.make_async_remote_copy(
            src_ref=ref, dst_ref=ref, send_sem=g_send, recv_sem=g_recv.at[l, group],
            device_id=targets[way], device_id_type=MESH,
        ).start()

    def await_all(ref, sem):
        pltpu.make_async_copy(ref, ref, sem).wait()

    def arrived(group, l):
        await_all(gath.at[l, pl.ds(0, BLOCKS[group] * ROWS)], g_recv.at[l, group])

    mine = pl.ds(pl.multiple_of(s_me * ROWS, 16), ROWS)

    def focus_copy(part, l):
        return pltpu.make_async_copy(
            focus.at[part, l], gath.at[l, mine, pl.ds(part * NPTS, NPTS)], f_sem
        )

    def refl_copy(part, l):
        return pltpu.make_async_copy(
            refl.at[part, l], mat.at[l, pl.ds(part * ROWS, ROWS)], r_sem
        )

    others = [
        pltpu.make_async_copy(a, b, loc_sem.at[i])
        for i, (a, b) in enumerate(((table, tab_v), (onset, on_v), (ending, end_v), (direct, dir_v)))
    ]
    barrier = pltpu.get_barrier_semaphore()
    for d in PEERS:
        pl.semaphore_signal(
            barrier, inc=1, device_id={"src": s_me, "freq": peer(d)}, device_id_type=MESH
        )
    for way in ("y", "z+", "z-"):
        pl.semaphore_signal(barrier, inc=1, device_id=targets[way], device_id_type=MESH)
    for l in range(L):
        for part in range(2):
            focus_copy(part, l).start()
    for l in range(L):
        for part in range(2):
            refl_copy(part, l).start()
    for c in others:
        c.start()
    await_all(gath.at[0, pl.ds(0, L * ROWS)], f_sem)
    pl.semaphore_wait(barrier, 3 + FRQ - 1)

    def phase(body):
        def step(l, carry):
            body(l)
            return carry

        lax.fori_loop(0, L, step, 0)

    def start_own(l):
        send(ZP1, l)
        send(ZM1, l)
        send(Y0, l)

    def near(l):
        arrived(OWN1, l)
        for k in (ZP2, ZM2, YM1, YP1):
            send(k, l)

    def second(l):
        arrived(OWN2, l)
        for k in (ZP3, ZM3):
            send(k, l)

    def third(l):
        arrived(OWN3, l)
        for k in (ZP4, ZM4, YM3, YP3):
            send(k, l)
        arrived(PAR1, l)
        for k in (ZQ2, ZN2):
            send(k, l)

    def fourth(l):
        arrived(OWN4, l)
        send(Y4, l)
        arrived(PAR2, l)
        for k in (ZQ3, ZN3):
            send(k, l)

    def piece_copy(d, l):
        return pltpu.make_async_remote_copy(
            src_ref=spec.at[l, pl.ds(pl.multiple_of(peer(d) * PIECE, 8), USED)],
            dst_ref=got.at[l, pl.ds(pl.multiple_of(f_me * PIECE, 8), USED)],
            send_sem=s_send, recv_sem=s_recv.at[l],
            device_id={"src": s_me, "freq": peer(d)}, device_id_type=MESH,
        )

    def own_piece(l):
        rows = pl.ds(pl.multiple_of(f_me * PIECE, 8), USED)
        return pltpu.make_async_copy(spec.at[l, rows], got.at[l, rows], s_recv.at[l])

    def product(l):
        arrived(REST, l)
        both = jnp.dot(mat[l], gath[l], preferred_element_type=jnp.float32)
        re = both[:ROWS, :NPTS] - both[ROWS:, NPTS:]
        im = both[:ROWS, NPTS:] + both[ROWS:, :NPTS]
        for p in (0, 8):
            rows = [slice(16 * j + p, 16 * j + p + 8) for j in range(PER)]
            largest = functools.reduce(
                jnp.maximum, [jnp.maximum(jnp.abs(re[r]), jnp.abs(im[r])) for r in rows]
            )
            code, *scale = block_scale(largest)
            words = [pack(to_int(re[r], scale), to_int(im[r], scale)) for r in rows]
            for j, word in enumerate(words + [code]):
                spec[l, pl.ds(p * PIECE + j, 8, stride=PIECE), :] = word
        own_piece(l).start()
        for d in PEERS:
            piece_copy(d, l).start()

    phase(start_own)
    phase(near)
    phase(second)
    phase(third)
    await_all(mat, r_sem)
    for c in others:
        c.wait()
    tab_a[...] = tab_v[:, :384].astype(jnp.bfloat16)
    tab_b[...] = tab_v[:, 384:].astype(jnp.bfloat16)

    def last(i, carry):
        @pl.when(i < L)
        def _():
            fourth(i)

        @pl.when(i >= LAG)
        def _():
            product(i - LAG)

        return carry

    lax.fori_loop(0, L + LAG, last, 0)

    def collect(l):
        await_all(got.at[l, pl.ds(0, FRQ * USED)], s_recv.at[l])

    def columns(j, l):
        word = got[l, pl.ds(j, FRQ, stride=PIECE), :]
        one, two = scale_of(got[l, pl.ds(PER, FRQ, stride=PIECE), :])
        high, low = split(
            jnp.concatenate(
                [part(word).astype(jnp.float32) * one * two for part in (first_of, second_of)], axis=0
            )
        )
        return jnp.concatenate([high, low, high], axis=0)

    def transform(tab, j, ls):
        js = range(j, min(j + 2, PER))
        cols = jnp.concatenate(
            [jnp.concatenate([columns(k, l) for l in ls], axis=0) for k in js], axis=1
        )
        result = jnp.dot(tab, cols, preferred_element_type=jnp.float32)
        return [(k, result[:, NPTS * i : NPTS * (i + 1)]) for i, k in enumerate(js)]

    for l in range(L - 1):
        collect(l)
    for j in range(0, PER, 2):
        for k, result in transform(tab_a[:, : 96 * (L - 1)], j, range(L - 1)):
            early[k] = result
    sample = lax.rem(128 - lax.broadcasted_iota(jnp.int32, (128, NPTS), 0), 128)
    collect(L - 1)
    largest = jnp.zeros((128, NPTS), jnp.float32)
    for j in range(0, PER, 2):
        for k, result in transform(tab_b[:, :96], j, (L - 1,)):
            r = pl.ds(16 * k + f_me, 1)
            window = (sample >= on_v[r, :]) & (sample < end_v[r, :])
            result = jnp.where(window, result + early[k], 0.0)
            early[k] = result
            largest = jnp.maximum(largest, jnp.abs(result))
    code, *scale = block_scale(largest)
    for j in range(0, PER, 2):
        word = pack(
            to_int(early[j], scale), to_int(early[j + 1], scale) if j + 1 < PER else code
        )
        for d in range(FRQ):
            trace[pl.ds(d * BACK + j * 4, 8), :] = word[8 * d : 8 * d + 8]

    rows = pl.ds(pl.multiple_of(f_me * BACK, 8), BACK)
    for d in PEERS:
        pltpu.make_async_remote_copy(
            src_ref=trace.at[pl.ds(pl.multiple_of(peer(d) * BACK, 8), BACK)],
            dst_ref=back.at[rows],
            send_sem=t_send, recv_sem=t_recv,
            device_id={"src": s_me, "freq": peer(d)}, device_id_type=MESH,
        ).start()
    pltpu.make_async_copy(trace.at[rows], back.at[rows], t_recv).start()
    await_all(back.at[pl.ds(0, FRQ * BACK)], t_recv)

    for t in range(8):
        for p in (0, 8):
            words = [
                back[pl.ds(p * BACK + i * 8 + t, 8, stride=BACK), :] for i in range((PER + 1) // 2)
            ]
            one, two = scale_of(second_of(words[-1]))
            for j in range(PER):
                value = (first_of, second_of)[j % 2](words[j // 2]).astype(jnp.float32)
                r = pl.ds(16 * j + p, 8)
                out[t, r, :] = dir_v[t, r, :] - value * one * two

    await_all(gath.at[:, pl.ds(0, SENT * ROWS)], g_send)
    await_all(spec.at[:, pl.ds(0, (FRQ - 1) * USED)], s_send)
    await_all(trace.at[pl.ds(0, (FRQ - 1) * BACK)], t_send)


def transform_table():
    device = np.arange(FRQ)
    reverse = sum(((device >> b) & 1) << (3 - b) for b in range(4))
    frequency = (np.arange(L)[:, None] * FRQ + reverse[None, :]).astype(np.int64)
    angle = (np.arange(128)[:, None, None] * frequency[None]) % 128 * (2.0 * np.pi / 128)
    full = np.stack([np.cos(angle), np.sin(angle)], axis=2).reshape(128, L, 32) / 8.0
    full = full.astype(np.float32)
    high = full.astype(ml_dtypes.bfloat16).astype(np.float32)
    low = (full - high).astype(ml_dtypes.bfloat16).astype(np.float32)
    three = np.concatenate([high, high, low], axis=2)
    table = np.zeros((128, 512), np.float32)
    table[:, : 96 * (L - 1)] = three[:, : L - 1].reshape(128, 96 * (L - 1))
    table[:, 384:480] = three[:, L - 1]
    return table


def per_device(reflection, focusing, direct_field, onset_index, end_index):
    f32, bf16 = jnp.float32, jnp.bfloat16
    dma = pltpu.SemaphoreType.DMA
    hbm = pl.BlockSpec(memory_space=pltpu.HBM)
    return pl.pallas_call(
        kernel,
        out_shape=pltpu.VMEM((8, ROWS, NPTS), f32),
        in_specs=[hbm] * 6,
        out_specs=pl.BlockSpec(memory_space=pltpu.VMEM),
        scratch_shapes=[
            pltpu.VMEM((L, NSRC, 2 * NPTS), bf16),
            pltpu.VMEM((L, 2 * ROWS, NSRC), bf16),
            pltpu.VMEM((L, (FRQ + 1) * PIECE, NPTS), jnp.int32),
            pltpu.VMEM((L, (FRQ + 1) * PIECE, NPTS), jnp.int32),
            pltpu.VMEM(((FRQ + 1) * BACK, NPTS), jnp.int32),
            pltpu.VMEM(((FRQ + 1) * BACK, NPTS), jnp.int32),
            pltpu.VMEM((8, ROWS, NPTS), f32),
            pltpu.VMEM((ROWS, NPTS), jnp.int32),
            pltpu.VMEM((ROWS, NPTS), jnp.int32),
            pltpu.VMEM((128, 512), f32),
            pltpu.VMEM((128, 384), bf16),
            pltpu.VMEM((128, 128), bf16),
            pltpu.VMEM((PER, 128, NPTS), f32),
            dma,
            dma((L, len(BLOCKS))),
            dma,
            dma((L,)),
            dma,
            dma,
            dma,
            dma,
            dma((4,)),
        ],
        compiler_params=pltpu.CompilerParams(
            collective_id=0, has_side_effects=True, vmem_limit_bytes=60 * 2**20
        ),
        name="marchenko",
    )(
        reflection, focusing, direct_field, onset_index, end_index,
        jnp.asarray(transform_table()),
    )


def solution(mesh):
    placed = (
        P(None, "freq", "src", None),
        P(None, "freq", "src", None),
        P("freq", "src", None),
        P("src", None),
        P("src", None),
    )
    return jax.shard_map(
        per_device, mesh=mesh, in_specs=placed, out_specs=P("freq", "src", None), check_vma=False
    )
```
